128 devices in a mesh: leaf: 128 (over x, z, y, core).
Axes of the slice: x: 4, y: 4, z: 4, core: 2. Of those that a mesh axis runs over, the one named last changes fastest.
Arguments:
- points: float32 [131072, 64], P('leaf'), may hold values from -6 to 6
- coefficients: float32 [131072, 256], P('leaf'), may hold values from -6 to 6
- leaf_skeleton: int32 [256, 256], P('leaf'), may hold values from 0 to 511, as said below
- node_skeleton: int32 [128, 256], P('leaf'), may hold values from 0 to 511, as said below
- pair_skeleton: int32 [64, 256], replicated, may hold values from 0 to 511, as said below
- quad_skeleton: int32 [32, 256], replicated, may hold values from 0 to 511, as said below
- top_skeleton: int32 [16, 256], replicated, may hold values from 0 to 511, as said below
- near_list: int32 [256, 3], P('leaf'), may hold values from -1 to 255, as said below
- far_list: int32 [128, 3], P('leaf'), may hold values from -1 to 127, as said below
- top_far_list: int32 [16, 3], replicated, may hold values from 0 to 15, as said below
Outputs:
- potential: float32 [131072, 256], P('leaf')
The draws below stay inside these ranges and needn't reach their ends.
Inputs may be any that keep to these rules, and one draw needn't show every extreme that they name: `leaf_skeleton`: each row holds 256 distinct rows of its leaf. `node_skeleton`: each row holds 256 distinct candidate rows. `pair_skeleton`: each row holds 256 distinct candidate rows. `quad_skeleton`: each row holds 256 distinct candidate rows. `top_skeleton`: each row holds 256 distinct candidate rows. `near_list`: row l names leaf l first; each other slot names a distinct leaf j with 1 <= |j - l| <= 2, or is -1. `far_list`: each slot names a distinct node m with 2 <= |m - n| <= 4, or is -1. `top_far_list`: each row names 3 distinct top nodes other than its own.
All inputs are finite; a program needn't handle non-finite values.
Results may differ from the reference program's by a relative error of at most 0.0003.
Values sent between devices are 32-bit elements; how exact they have to be, the bound alone decides.
A program may use at most 128 MiB of HBM per device.

```python
import jax
import jax.numpy as jnp
from jax import lax

FEAT = 64
RHS = 256
RANK = 256
LEAF = 512
NEAR = 3
FAR1 = 3
FAR4 = 3
REACH = 4
NODES = 128
LEAVES = 256
POINTS = 131072
PAIRS = 64
QUADS = 32
TOPS = 16


def distinct_rows(key, rows, span):

    def single_row(row_key):
        return jax.random.permutation(row_key, span)[:RANK]
    return jax.vmap(single_row)(jax.random.split(key, rows)).astype(jnp.int32)


def draw_leaf_skeleton(key, part):
    return distinct_rows(jax.random.fold_in(key, 11), LEAVES, LEAF)


def draw_node_skeleton(key, part):
    return distinct_rows(jax.random.fold_in(key, 12), NODES, 2 * RANK)


def draw_pair_skeleton(key, part):
    return distinct_rows(jax.random.fold_in(key, 13), PAIRS, 2 * RANK)


def draw_quad_skeleton(key, part):
    return distinct_rows(jax.random.fold_in(key, 14), QUADS, 2 * RANK)


def draw_top_skeleton(key, part):
    return distinct_rows(jax.random.fold_in(key, 15), TOPS, 2 * RANK)


def pick_offsets(key, rows, offsets, slots):
    width = offsets.shape[0]
    scores = jax.random.randint(key, (rows, width), 0, 65536) * width + jnp.arange(width, dtype=jnp.int32)[None, :]
    order = jnp.argsort(scores, axis=1)
    return offsets[order][:, :slots]


def draw_near_list(key, part):
    offsets = jnp.array([-2, -1, 1, 2], dtype=jnp.int32)
    chosen = pick_offsets(jax.random.fold_in(key, 21), LEAVES, offsets, NEAR - 1)
    leaf_ids = jnp.arange(LEAVES, dtype=jnp.int32)
    heavy_shift = jax.random.randint(jax.random.fold_in(key, 22), (), 0, 8)
    heavy = (leaf_ids // 2 + heavy_shift) % 8 == 0
    light_counts = jax.random.randint(jax.random.fold_in(key, 23), (LEAVES,), 0, NEAR - 1)
    counts = jnp.where(heavy, NEAR - 1, light_counts)
    targets = leaf_ids[:, None] + chosen
    slots = jnp.arange(NEAR - 1, dtype=jnp.int32)[None, :]
    present = (slots < counts[:, None]) & (targets >= 0) & (targets < LEAVES)
    entries = jnp.where(present, targets, -1)
    return jnp.concatenate([leaf_ids[:, None], entries], axis=1).astype(jnp.int32)


def draw_far_list(key, part):
    offsets = jnp.concatenate([jnp.arange(-REACH, -1, dtype=jnp.int32), jnp.arange(2, REACH + 1, dtype=jnp.int32)])
    chosen = pick_offsets(jax.random.fold_in(key, 31), NODES, offsets, FAR1)
    node_ids = jnp.arange(NODES, dtype=jnp.int32)
    targets = node_ids[:, None] + chosen
    inside = (targets >= 0) & (targets < NODES)
    rank_inside = jnp.cumsum(inside.astype(jnp.int32), axis=1)
    counts = jax.random.randint(jax.random.fold_in(key, 32), (NODES,), 1, FAR1 + 1)
    present = inside & (rank_inside <= counts[:, None])
    return jnp.where(present, targets, -1).astype(jnp.int32)


def draw_top_far_list(key, part):
    scores = jax.random.randint(jax.random.fold_in(key, 41), (TOPS, TOPS), 0, 65536) * TOPS + jnp.arange(TOPS, dtype=jnp.int32)[None, :]
    own_node = jnp.arange(TOPS, dtype=jnp.int32)[:, None] == jnp.arange(TOPS, dtype=jnp.int32)[None, :]
    scores = jnp.where(own_node, 65536 * TOPS + TOPS, scores)
    order = jnp.argsort(scores, axis=1)
    return order[:, :FAR4].astype(jnp.int32)


def levels(rng, dims, pieces, least, top_value):
    level = 1.0
    for position, shards_of in pieces:
        steps = jax.random.uniform(jax.random.fold_in(jax.random.fold_in(rng, 6), position), (shards_of,), jnp.float32, least / len(pieces), top_value / len(pieces))
        level = level * jnp.repeat(jnp.exp(steps), dims[position] // shards_of).reshape((-1,) + (1,) * (len(dims) - 1 - position))
    return level


def noise(stream_key, extent, scale, reach, pieces=(), kind=jnp.bfloat16):
    factor_of = levels(stream_key, extent, pieces, -0.22, 0.18) if pieces else 1.0
    values = jax.random.normal(stream_key, extent, jnp.float32) * scale * factor_of
    return jnp.minimum(jnp.maximum(values, -reach), reach).astype(kind)


def setup_inputs(seed: int = 0) -> dict:
    arg_keys = jax.random.split(jax.random.key(seed), 11)
    return {
        "points": noise(arg_keys[0], (POINTS, FEAT), 1.0, 6.0, ((0, 128),), jnp.float32),
        "coefficients": noise(arg_keys[1], (POINTS, RHS), 1.0, 6.0, ((0, 128),), jnp.float32),
        "leaf_skeleton": draw_leaf_skeleton(jax.random.fold_in(arg_keys[10], 71), 0),
        "node_skeleton": draw_node_skeleton(jax.random.fold_in(arg_keys[10], 71), 0),
        "pair_skeleton": draw_pair_skeleton(jax.random.fold_in(arg_keys[10], 71), 0),
        "quad_skeleton": draw_quad_skeleton(jax.random.fold_in(arg_keys[10], 71), 0),
        "top_skeleton": draw_top_skeleton(jax.random.fold_in(arg_keys[10], 71), 0),
        "near_list": draw_near_list(jax.random.fold_in(arg_keys[10], 71), 0),
        "far_list": draw_far_list(jax.random.fold_in(arg_keys[10], 71), 0),
        "top_far_list": draw_top_far_list(jax.random.fold_in(arg_keys[10], 71), 0),
    }


HIGHEST = lax.Precision.HIGHEST


def square_distance(left_points, right_points):
    inner_product = jnp.dot(left_points, right_points.T, precision=HIGHEST, preferred_element_type=jnp.float32)
    return jnp.sum(left_points * left_points, 1)[:, None] + jnp.sum(right_points * right_points, 1)[None, :] - 2.0 * inner_product


def gaussian(left_points, right_points):
    return jnp.exp(-square_distance(left_points, right_points) / FEAT)


def interpolation(candidates, chosen_points):
    distances = square_distance(candidates, chosen_points)
    weights = jnp.exp(-3.0 * (distances - jnp.min(distances, axis=1, keepdims=True)) / FEAT)
    return weights / jnp.sum(weights, axis=1, keepdims=True)


def merge_level(candidates, child_values, skeleton):
    picked = jnp.take_along_axis(candidates, skeleton[:, :, None], axis=1)
    transfer = jax.vmap(interpolation)(candidates, picked)
    values = jnp.einsum('nkr,nkc->nrc', transfer, child_values, precision=HIGHEST)
    return picked, transfer, values


def reference(points, coefficients, leaf_skeleton, node_skeleton, pair_skeleton, quad_skeleton, top_skeleton, near_list, far_list, top_far_list):
    leaf_points = points.reshape(LEAVES, LEAF, FEAT)
    leaf_values = coefficients.reshape(LEAVES, LEAF, RHS)
    leaf_picked, leaf_basis, leaf_weights = merge_level(leaf_points, leaf_values, leaf_skeleton)
    level_points = leaf_picked
    level_values = leaf_weights
    transfers = []
    first_level = []
    for skeleton in (node_skeleton, pair_skeleton, quad_skeleton, top_skeleton):
        node_count = skeleton.shape[0]
        level_points, transfer, level_values = merge_level(level_points.reshape(node_count, 2 * RANK, FEAT), level_values.reshape(node_count, 2 * RANK, RHS), skeleton)
        transfers.append(transfer)
        if len(first_level) == 0:
            first_level = [level_points, level_values]
    node_points, node_values = first_level[0], first_level[1]
    node_far = jnp.zeros((NODES, RANK, RHS), jnp.float32)
    for slot_index in range(FAR1):
        source = far_list[:, slot_index]
        present = source >= 0
        safe_index = jnp.where(present, source, 0).astype(jnp.int32)
        kernel_tiles = jax.vmap(gaussian)(node_points, node_points[safe_index])
        contribution = jnp.einsum('nrk,nkc->nrc', kernel_tiles, node_values[safe_index], precision=HIGHEST)
        node_far = node_far + jnp.where(present[:, None, None], contribution, 0.0)
    top_field = jnp.zeros((TOPS, RANK, RHS), jnp.float32)
    for slot_index in range(FAR4):
        source = top_far_list[:, slot_index]
        kernel_tiles = jax.vmap(gaussian)(level_points, level_points[source])
        top_field = top_field + jnp.einsum('nrk,nkc->nrc', kernel_tiles, level_values[source], precision=HIGHEST)
    far_field = top_field
    for transfer in (transfers[3], transfers[2], transfers[1]):
        far_field = jnp.einsum('nkr,nrc->nkc', transfer, far_field, precision=HIGHEST).reshape(-1, RANK, RHS)
    far_field = far_field + node_far
    far_field = jnp.einsum('nkr,nrc->nkc', transfers[0], far_field, precision=HIGHEST).reshape(LEAVES, RANK, RHS)
    leaf_output = jnp.einsum('lpr,lrc->lpc', leaf_basis, far_field, precision=HIGHEST)

    def near_leaf(inputs):
        leaf_index, listed = inputs
        own_points = lax.dynamic_index_in_dim(leaf_points, leaf_index, 0, keepdims=False)
        running = jnp.zeros((LEAF, RHS), jnp.float32)
        for slot_index in range(NEAR):
            partner_leaf = listed[slot_index]
            present = partner_leaf >= 0
            safe_index = jnp.where(present, partner_leaf, 0).astype(jnp.int32)

            def compute_tile():
                other_points = lax.dynamic_index_in_dim(leaf_points, safe_index, 0, keepdims=False)
                other_values = lax.dynamic_index_in_dim(leaf_values, safe_index, 0, keepdims=False)
                return jnp.dot(gaussian(own_points, other_points), other_values, precision=HIGHEST, preferred_element_type=jnp.float32)

            def empty_tile():
                return jnp.zeros((LEAF, RHS), jnp.float32)

            running = running + lax.cond(present, compute_tile, empty_tile)
        return running

    near_part = lax.map(near_leaf, (jnp.arange(LEAVES, dtype=jnp.int32), near_list))
    return (leaf_output + near_part).reshape(POINTS, RHS)
```

```python
import math

import jax
import jax.numpy as jnp
from jax import lax
from jax.experimental import pallas as pl
from jax.experimental.pallas import tpu as pltpu
from jax.sharding import PartitionSpec as P

FEAT = 64
RHS = 256
RANK = 256
LEAF = 512
NEAR = 3
FAR1 = 3
FAR4 = 3
GROUP = 8
TOPS = 16
DEVICES = 128
SHARE = RHS // GROUP
HALF = RANK // 2

MESH = pl.DeviceIdType.MESH
F32 = jnp.float32
BF16 = jnp.bfloat16
SCALE = math.sqrt(2.0 * math.log2(math.e) / FEAT)


def dot(left, right, dims):
    return lax.dot_general(left, right, (dims, ((), ())), preferred_element_type=F32)


def nn(left, right):
    return dot(left, right, ((1,), (0,)))


def nt(left, right):
    return dot(left, right, ((1,), (1,)))


def tn(left, right):
    return dot(left, right, ((0,), (0,)))


def split(values):
    high = values.astype(BF16)
    low = (values - high.astype(F32)).astype(BF16)
    return high, low


def product3(mul, left, right):
    return mul(left[0], right[0]) + (mul(left[0], right[1]) + mul(left[1], right[0]))


def thin_product(mul, left, right):
    rows = left.shape[0]
    high, low = split(left)
    both = mul(jnp.concatenate([high, low], axis=0), right[0])
    return both[:rows] + (both[rows:] + mul(high, right[1]))


def lanes_of(shape):
    return lax.broadcasted_iota(jnp.int32, shape, 1)


def swap_halves(tile):
    return pltpu.roll(tile, FEAT, 1)


def doubled(packed):
    lane = lanes_of(packed.shape)
    swapped = swap_halves(packed)
    return jnp.concatenate(
        [jnp.where(lane < FEAT, packed, swapped), jnp.where(lane < FEAT, swapped, packed)], axis=0
    )


def forms(twice):
    lane = lanes_of(twice.shape)
    first = lane < FEAT
    high = twice.astype(BF16).astype(F32)
    low = twice - high
    norm = -0.25 * jnp.sum(twice * twice, axis=1, keepdims=True)
    norm1 = norm.astype(BF16).astype(F32)
    norm2 = (norm - norm1).astype(BF16).astype(F32)
    norm3 = norm - norm1 - norm2

    def placed(base):
        return jnp.where(
            lane == base, norm1, jnp.where(lane == base + 1, norm2, jnp.where(lane == base + 2, norm3, 0.0))
        )

    ones_left = jnp.where((lane >= FEAT + 3) & (lane < FEAT + 6), 1.0, placed(FEAT))
    ones_right = jnp.where((lane >= FEAT) & (lane < FEAT + 3), 1.0, placed(FEAT + 3))
    left = jnp.concatenate(
        [jnp.where(first, high, low).astype(BF16), jnp.where(first, high, ones_left).astype(BF16)], axis=1
    )
    right = jnp.concatenate(
        [jnp.where(first, low, high).astype(BF16), jnp.where(first, high, ones_right).astype(BF16)], axis=1
    )
    return left, right


def picked_forms(picked):
    head, tail = picked[:, :128], picked[:, 128:]
    lane = lanes_of(head.shape)
    swapped = swap_halves(head)
    moved = pltpu.roll(tail, 3, 1)
    tail_right = jnp.where(
        lane < FEAT,
        tail,
        jnp.where(lane < FEAT + 3, 1.0, jnp.where(lane < FEAT + 6, moved, 0.0)),
    )
    right = jnp.concatenate([swapped.astype(BF16), tail_right.astype(BF16)], axis=1)
    return picked.astype(BF16), right, head + swapped


def one_hot(column):
    spread = lax.broadcasted_iota(jnp.int32, (RANK, 2 * RANK), 1)
    return jnp.where(spread == column, 1.0, 0.0).astype(BF16)


def softmax3(exponent):
    top = jnp.max(exponent, axis=1, keepdims=True)
    weights = jnp.exp2(3.0 * (exponent - top))
    return weights / jnp.sum(weights, axis=1, keepdims=True)


def kernel(
    near_list,
    far_list,
    top_far_list,
    points,
    coefficients,
    leaf_skeleton,
    node_skeleton,
    pair_skeleton,
    quad_skeleton,
    top_skeleton,
    out,
    near_send_points,
    near_points,
    near_values,
    node_points,
    node_values,
    node_lists,
    list_scalars,
    top_points,
    top_values,
    field_out,
    field_in,
    weights_t,
    index_rows,
    index_columns,
    leaf_left,
    near_right,
    values_high,
    values_low,
    basis_high,
    basis_low,
    node_left,
    node_right,
    upper_left,
    upper_right,
    pair_high,
    pair_low,
    chain_high,
    chain_low,
    near_send,
    near_recv,
    gpts_send,
    gpts_recv,
    glist_send,
    glist_recv,
    gval_send,
    gval_recv,
    edge_send,
    edge_recv,
    tpts_send,
    tpts_recv,
    tval_send,
    tval_recv,
    back_send,
    back_recv,
    local_sem,
):
    me = lax.axis_index("leaf")
    place = lax.rem(me, GROUP)
    group = me // GROUP
    right_device = lax.rem(me + 1, DEVICES)
    left_device = lax.rem(me + DEVICES - 1, DEVICES)
    next_group = lax.rem(group + 1, TOPS) * GROUP + place
    previous_group = lax.rem(group + TOPS - 1, TOPS) * GROUP + place

    def mate(step):
        return group * GROUP + lax.rem(place + step, GROUP)

    def peer(step):
        return lax.rem(group + step, TOPS) * GROUP + place

    barrier = pltpu.get_barrier_semaphore()
    partners = [right_device, left_device]
    partners += [mate(step) for step in range(1, GROUP)]
    partners += [peer(step) for step in range(1, TOPS)]
    for partner in partners:
        pl.semaphore_signal(barrier, inc=1, device_id=(partner,), device_id_type=MESH)

    def remote(source, target, send, recv, device):
        return pltpu.make_async_remote_copy(
            src_ref=source, dst_ref=target, send_sem=send, recv_sem=recv, device_id=(device,), device_id_type=MESH
        )

    started = []

    def start(*args):
        copy = remote(*args)
        copy.start()
        started.append(copy)

    near_send_points[...] = jnp.concatenate([points[0:LEAF, :], points[LEAF : 2 * LEAF, :]], axis=1) * SCALE
    pl.semaphore_wait(barrier, len(partners))

    def near_copies():
        copies = []
        for side, device in ((0, right_device), (1, left_device)):
            copies.append((near_send_points, near_points.at[side], near_send.at[side, 0], near_recv.at[side, 0], device))
            for part in range(4):
                rows = pl.ds(part * 256, 256)
                copies.append(
                    (
                        coefficients.at[rows, :],
                        near_values.at[side, rows, :],
                        near_send.at[side, part + 1],
                        near_recv.at[side, part + 1],
                        device,
                    )
                )
        return copies

    for copy in near_copies():
        start(*copy)

    index_rows[...] = jnp.zeros_like(index_rows)
    index_rows[0:2, :] = leaf_skeleton[...].astype(F32)
    index_rows[2:3, :] = node_skeleton[...].astype(F32)
    for i in range(4):
        index_rows[3 + i : 4 + i, :] = pair_skeleton[pl.ds(group * 4 + i, 1), :].astype(F32)
    for i in range(2):
        index_rows[7 + i : 8 + i, :] = quad_skeleton[pl.ds(group * 2 + i, 1), :].astype(F32)
    index_rows[9:10, :] = top_skeleton[pl.ds(group, 1), :].astype(F32)
    index_columns[...] = jnp.transpose(index_rows[...]).astype(jnp.int32)

    def chosen(number):
        return one_hot(index_columns[:, number : number + 1])

    leaf_picks = []
    for leaf in range(2):
        packed = near_send_points[...]
        lane = lanes_of(packed.shape)
        swapped = swap_halves(packed)
        twice = jnp.where(lane < FEAT, packed, swapped) if leaf == 0 else jnp.where(lane < FEAT, swapped, packed)
        left, right = forms(twice)
        leaf_left[leaf * LEAF : (leaf + 1) * LEAF, :] = left
        near_right[2 + leaf] = right
        pick_left, pick_right, _ = picked_forms(nn(chosen(leaf), left))
        upper_left[leaf * RANK : (leaf + 1) * RANK, :] = pick_left
        upper_right[leaf * RANK : (leaf + 1) * RANK, :] = pick_right
    _, node_pick_right, node_twice = picked_forms(nn(chosen(2), upper_left[0 : 2 * RANK, :]))
    lane = lanes_of((HALF, 128))
    node_points[4 + place] = jnp.where(lane < FEAT, node_twice[:HALF], node_twice[HALF:])
    lane_row = lanes_of((1, 128))
    node_lists[place] = jnp.where(
        lane_row == 0, far_list[0, 0], jnp.where(lane_row == 1, far_list[0, 1], far_list[0, 2])
    )
    for step in range(1, GROUP):
        start(
            node_points.at[4 + place], node_points.at[4 + place], gpts_send.at[step], gpts_recv.at[step], mate(step)
        )
    for step in range(1, GROUP):
        start(node_lists.at[place], node_lists.at[place], glist_send.at[step], glist_recv.at[step], mate(step))

    for leaf in range(2):
        rows = slice(leaf * LEAF, (leaf + 1) * LEAF)
        picks = slice(leaf * RANK, (leaf + 1) * RANK)
        basis = softmax3(nt(leaf_left[rows, :], upper_right[picks, :]))
        transfer = softmax3(nt(upper_left[picks, :], node_pick_right))
        high, low = split(product3(nn, split(basis), split(transfer)))
        basis_high[rows, :] = high
        basis_low[rows, :] = low
        high, low = split(coefficients[rows, :])
        values_high[2 + leaf] = high
        values_low[2 + leaf] = low
    weights = product3(
        tn,
        (values_high[2:4].reshape(2 * LEAF, RHS), values_low[2:4].reshape(2 * LEAF, RHS)),
        (basis_high[...], basis_low[...]),
    )
    weights_t[...] = weights.reshape(GROUP, SHARE, RANK)
    for step in range(1, GROUP):
        start(
            weights_t.at[lax.rem(place + step, GROUP)],
            node_values.at[4 + place],
            gval_send.at[step],
            gval_recv.at[step],
            mate(step),
        )
    node_values[4 + place] = weights_t[place]

    for step in range(1, GROUP):
        source = 4 + lax.rem(place + GROUP - step, GROUP)
        remote(
            node_points.at[source], node_points.at[source], gpts_send.at[step], gpts_recv.at[step], mate(step)
        ).wait_recv()
    start(node_points.at[pl.ds(8, 4)], node_points.at[pl.ds(0, 4)], edge_send.at[0], edge_recv.at[0], next_group)
    start(node_points.at[pl.ds(4, 4)], node_points.at[pl.ds(12, 4)], edge_send.at[1], edge_recv.at[1], previous_group)

    def node_forms(node, carry):
        left, right = forms(doubled(node_points[node]))
        node_left[node] = left
        node_right[node] = right
        return carry

    lax.fori_loop(4, 12, node_forms, 0)

    for pair in range(4):
        rows = slice(pair * RANK, (pair + 1) * RANK)
        below = node_left[4 + 2 * pair : 6 + 2 * pair].reshape(2 * RANK, 256)
        upper_left[rows, :], upper_right[rows, :], _ = picked_forms(nn(chosen(3 + pair), below))
    for quad in range(2):
        rows = slice((4 + quad) * RANK, (5 + quad) * RANK)
        below = slice(2 * quad * RANK, (2 * quad + 2) * RANK)
        upper_left[rows, :], upper_right[rows, :], _ = picked_forms(nn(chosen(7 + quad), upper_left[below, :]))
    _, upper_right[6 * RANK : 7 * RANK, :], top_twice = picked_forms(
        nn(chosen(9), upper_left[4 * RANK : 6 * RANK, :])
    )
    lane = lanes_of((HALF, 128))
    top_points[group] = jnp.where(lane < FEAT, top_twice[:HALF], top_twice[HALF:])
    for step in range(1, TOPS):
        start(top_points.at[group], top_points.at[group], tpts_send.at[step], tpts_recv.at[step], peer(step))

    top_transfer = softmax3(nt(upper_left[4 * RANK : 6 * RANK, :], upper_right[6 * RANK : 7 * RANK, :]))
    for quad in range(2):
        below = slice(2 * quad * RANK, (2 * quad + 2) * RANK)
        transfer = softmax3(nt(upper_left[below, :], upper_right[(4 + quad) * RANK : (5 + quad) * RANK, :]))
        chain = product3(nn, split(transfer), split(top_transfer[quad * RANK : (quad + 1) * RANK]))
        pair_high[below, :], pair_low[below, :] = split(chain)

    def pair_chain(pair, carry):
        rows = pl.ds(pl.multiple_of(pair * RANK, RANK), RANK)
        store = pl.ds(pl.multiple_of(2 * pair * RANK, RANK), 2 * RANK)
        transfer = softmax3(nt(node_left[pl.ds(2 * pair + 4, 2)].reshape(2 * RANK, 256), upper_right[rows, :]))
        chain = product3(nn, split(transfer), (pair_high[rows, :], pair_low[rows, :]))
        chain_high[store, :], chain_low[store, :] = split(chain)
        return carry

    lax.fori_loop(0, 4, pair_chain, 0)

    for step in range(1, GROUP):
        source = 4 + lax.rem(place + GROUP - step, GROUP)
        remote(
            weights_t.at[0], node_values.at[source], gval_send.at[step], gval_recv.at[step], mate(step)
        ).wait_recv()
    start(node_values.at[pl.ds(8, 4)], node_values.at[pl.ds(0, 4)], edge_send.at[2], edge_recv.at[2], next_group)
    start(node_values.at[pl.ds(4, 4)], node_values.at[pl.ds(12, 4)], edge_send.at[3], edge_recv.at[3], previous_group)

    def lift(node, total):
        rows = pl.ds(pl.multiple_of(node * RANK, RANK), RANK)
        return total + thin_product(nn, node_values[4 + node], (chain_high[rows, :], chain_low[rows, :]))

    top_values[group] = lax.fori_loop(0, GROUP, lift, jnp.zeros((SHARE, RANK), F32))
    for step in range(1, TOPS):
        start(top_values.at[group], top_values.at[group], tval_send.at[step], tval_recv.at[step], peer(step))

    def near_tile(leaf, half, position):
        rows = pl.ds(pl.multiple_of(leaf * LEAF + half * 256, 256), 256)
        tile = split(jnp.exp2(nt(leaf_left[rows, :], near_right[position])))
        return rows, product3(nn, tile, (values_high[position], values_low[position]))

    def own_tile(step, carry):
        leaf = step // 2
        rows, value = near_tile(leaf, step % 2, 2 + leaf)
        out[rows, :] = value
        return carry

    lax.fori_loop(0, 4, own_tile, 0)

    for step in range(1, GROUP):
        source = lax.rem(place + GROUP - step, GROUP)
        remote(
            node_lists.at[source], node_lists.at[source], glist_send.at[step], glist_recv.at[step], mate(step)
        ).wait_recv()
    to_scalars = pltpu.make_async_copy(node_lists, list_scalars, local_sem)
    to_scalars.start()
    to_scalars.wait()
    for side, target in ((0, 0), (1, 12)):
        landed = node_points.at[pl.ds(target, 4)]
        remote(landed, landed, edge_send.at[side], edge_recv.at[side], next_group).wait_recv()
    lax.fori_loop(0, 4, node_forms, 0)
    lax.fori_loop(12, 16, node_forms, 0)
    for side, target in ((0, 0), (1, 12)):
        landed = node_values.at[pl.ds(target, 4)]
        remote(landed, landed, edge_send.at[2 + side], edge_recv.at[2 + side], next_group).wait_recv()

    def far_node(node, carry):
        mine_right = node_right[4 + node]
        total = jnp.zeros((SHARE, RANK), F32)
        for slot in range(FAR1):
            entry = list_scalars[node, 0, slot]
            weight = (jnp.minimum(entry, 0) + 1).astype(F32)
            position = jnp.maximum(entry - group * GROUP + 4, 0)
            tile = split(jnp.exp2(nt(node_left[position], mine_right)))
            total = total + weight * thin_product(nn, node_values[position], tile)
        field_out[node] = total
        return carry

    lax.fori_loop(0, GROUP, far_node, 0)

    for step in range(1, TOPS):
        source = lax.rem(group + TOPS - step, TOPS)
        remote(
            top_points.at[source], top_points.at[source], tpts_send.at[step], tpts_recv.at[step], peer(step)
        ).wait_recv()
    for step in range(1, TOPS):
        source = lax.rem(group + TOPS - step, TOPS)
        remote(
            top_values.at[source], top_values.at[source], tval_send.at[step], tval_recv.at[step], peer(step)
        ).wait_recv()
    top_field = jnp.zeros((SHARE, RANK), F32)
    for slot in range(FAR4):
        source = top_far_list[group, slot]
        left, _ = forms(doubled(top_points[source]))
        tile = split(jnp.exp2(nt(left, upper_right[6 * RANK : 7 * RANK, :])))
        top_field = top_field + thin_product(nn, top_values[source], tile)
    for node in range(GROUP):
        rows = slice(node * RANK, (node + 1) * RANK)
        field_out[node] = field_out[node] + thin_product(nt, top_field, (chain_high[rows, :], chain_low[rows, :]))
    for step in range(1, GROUP):
        start(
            field_out.at[lax.rem(place + step, GROUP)],
            field_in.at[place],
            back_send.at[step],
            back_recv.at[step],
            mate(step),
        )
    field_in[place] = field_out[place]

    for side in range(2):
        for part in range(5):
            if part == 0:
                landed = near_points.at[side]
            else:
                landed = near_values.at[side, pl.ds((part - 1) * 256, 256), :]
            remote(landed, landed, near_send.at[side, part], near_recv.at[side, part], right_device).wait_recv()
        packed = near_points[side]
        lane = lanes_of(packed.shape)
        swapped = swap_halves(packed)
        for leaf in range(2):
            twice = jnp.where(lane < FEAT, packed, swapped) if leaf == 0 else jnp.where(lane < FEAT, swapped, packed)
            slot = 4 * side + leaf
            _, near_right[slot] = forms(twice)
            values_high[slot], values_low[slot] = split(near_values[side, leaf * LEAF : (leaf + 1) * LEAF, :])

    def other_tile(step, carry):
        leaf = step // 4
        slot = 1 + (step % 4) // 2
        entry = near_list[leaf, slot]
        position = jnp.maximum(entry - 2 * me + 2, 0)
        weight = (jnp.minimum(entry, 0) + 1).astype(F32)
        rows, value = near_tile(leaf, step % 2, position)
        out[rows, :] = out[rows, :] + weight * value
        return carry

    lax.fori_loop(0, 8, other_tile, 0)

    for step in range(1, GROUP):
        source = lax.rem(place + GROUP - step, GROUP)
        remote(
            field_out.at[0], field_in.at[source], back_send.at[step], back_recv.at[step], mate(step)
        ).wait_recv()
    field = split(field_in[...].reshape(RHS, RANK))

    def finish(step, carry):
        rows = pl.ds(pl.multiple_of(step * 256, 256), 256)
        out[rows, :] = out[rows, :] + product3(nt, (basis_high[rows, :], basis_low[rows, :]), field)
        return carry

    lax.fori_loop(0, 4, finish, 0)
    for copy in started:
        copy.wait_send()


def body(
    points,
    coefficients,
    leaf_skeleton,
    node_skeleton,
    pair_skeleton,
    quad_skeleton,
    top_skeleton,
    near_list,
    far_list,
    top_far_list,
):
    vmem = pl.BlockSpec(memory_space=pltpu.VMEM)
    smem = pl.BlockSpec(memory_space=pltpu.SMEM)
    dma = pltpu.SemaphoreType.DMA
    return pl.pallas_call(
        kernel,
        out_shape=jax.ShapeDtypeStruct((2 * LEAF, RHS), F32),
        in_specs=[smem] * 3 + [vmem] * 7,
        out_specs=vmem,
        scratch_shapes=[
            pltpu.VMEM((LEAF, 128), F32),
            pltpu.VMEM((2, LEAF, 128), F32),
            pltpu.VMEM((2, 2 * LEAF, RHS), F32),
            pltpu.VMEM((16, HALF, 128), F32),
            pltpu.VMEM((16, SHARE, RANK), F32),
            pltpu.VMEM((GROUP, 1, 128), jnp.int32),
            pltpu.SMEM((GROUP, 1, 128), jnp.int32),
            pltpu.VMEM((TOPS, HALF, 128), F32),
            pltpu.VMEM((TOPS, SHARE, RANK), F32),
            pltpu.VMEM((GROUP, SHARE, RANK), F32),
            pltpu.VMEM((GROUP, SHARE, RANK), F32),
            pltpu.VMEM((GROUP, SHARE, RANK), F32),
            pltpu.VMEM((128, RANK), F32),
            pltpu.VMEM((RANK, 128), jnp.int32),
            pltpu.VMEM((2 * LEAF, 256), BF16),
            pltpu.VMEM((6, LEAF, 256), BF16),
            pltpu.VMEM((6, LEAF, RHS), BF16),
            pltpu.VMEM((6, LEAF, RHS), BF16),
            pltpu.VMEM((2 * LEAF, RANK), BF16),
            pltpu.VMEM((2 * LEAF, RANK), BF16),
            pltpu.VMEM((16, RANK, 256), BF16),
            pltpu.VMEM((16, RANK, 256), BF16),
            pltpu.VMEM((7 * RANK, 256), BF16),
            pltpu.VMEM((7 * RANK, 256), BF16),
            pltpu.VMEM((4 * RANK, RANK), BF16),
            pltpu.VMEM((4 * RANK, RANK), BF16),
            pltpu.VMEM((8 * RANK, RANK), BF16),
            pltpu.VMEM((8 * RANK, RANK), BF16),
            dma((2, 5)),
            dma((2, 5)),
            dma((GROUP,)),
            dma((GROUP,)),
            dma((GROUP,)),
            dma((GROUP,)),
            dma((GROUP,)),
            dma((GROUP,)),
            dma((4,)),
            dma((4,)),
            dma((TOPS,)),
            dma((TOPS,)),
            dma((TOPS,)),
            dma((TOPS,)),
            dma((GROUP,)),
            dma((GROUP,)),
            dma,
        ],
        compiler_params=pltpu.CompilerParams(
            collective_id=0, has_side_effects=True, vmem_limit_bytes=56 * 1024 * 1024
        ),
    )(
        near_list,
        far_list,
        top_far_list,
        points,
        coefficients,
        leaf_skeleton,
        node_skeleton,
        pair_skeleton,
        quad_skeleton,
        top_skeleton,
    )


def solution(mesh):
    return jax.shard_map(
        body,
        mesh=mesh,
        in_specs=(
            P("leaf", None),
            P("leaf", None),
            P("leaf", None),
            P("leaf", None),
            P(),
            P(),
            P(),
            P("leaf", None),
            P("leaf", None),
            P(),
        ),
        out_specs=P("leaf", None),
        check_vma=False,
    )
```

```python
import math

import jax
import jax.numpy as jnp
from jax import lax
from jax.experimental import pallas as pl
from jax.experimental.pallas import tpu as pltpu
from jax.sharding import PartitionSpec as P

FEAT = 64
RHS = 256
RANK = 256
LEAF = 512
NEAR = 3
FAR1 = 3
FAR4 = 3
GROUP = 8
TOPS = 16
DEVICES = 128
SHARE = RHS // GROUP
HALF = RANK // 2

MESH = pl.DeviceIdType.MESH
F32 = jnp.float32
BF16 = jnp.bfloat16
SCALE = math.sqrt(2.0 * math.log2(math.e) / FEAT)


def dot(left, right, dims):
    return lax.dot_general(left, right, (dims, ((), ())), preferred_element_type=F32)


def nn(left, right):
    return dot(left, right, ((1,), (0,)))


def nt(left, right):
    return dot(left, right, ((1,), (1,)))


def tn(left, right):
    return dot(left, right, ((0,), (0,)))


def split(values):
    high = values.astype(BF16)
    low = (values - high.astype(F32)).astype(BF16)
    return high, low


def product3(mul, left, right):
    return mul(left[0], right[0]) + (mul(left[0], right[1]) + mul(left[1], right[0]))


def thin_product(mul, left, right):
    rows = left.shape[0]
    high, low = split(left)
    both = mul(jnp.concatenate([high, low], axis=0), right[0])
    return both[:rows] + (both[rows:] + mul(high, right[1]))


def parts(points):
    high = points.astype(BF16).astype(F32)
    low = points - high
    norm = -0.5 * jnp.sum(points * points, axis=0, keepdims=True)
    norm1 = norm.astype(BF16).astype(F32)
    norm2 = (norm - norm1).astype(BF16).astype(F32)
    norm3 = norm - norm1 - norm2
    row = lax.broadcasted_iota(jnp.int32, (16, points.shape[1]), 0)
    norms = jnp.where(row == 0, norm1, jnp.where(row == 1, norm2, jnp.where(row == 2, norm3, 0.0)))
    ones = jnp.where(row < 3, 1.0, 0.0)
    rest = jnp.zeros((32, points.shape[1]), F32)
    return high, low, norms, ones, rest


def right_form(points):
    high, low, norms, ones, rest = parts(points)
    return jnp.concatenate([low, high, high, ones, norms, rest], axis=0).astype(BF16)


def left_of(right):
    return jnp.concatenate(
        [right[64:128], right[0:64], right[128:192], right[208:224], right[192:208], right[224:256]], axis=0
    )


def exponents(left_points, right_points):
    return tn(left_of(left_points), right_points)


def pick(candidates, table_row):
    spread = lax.broadcasted_iota(jnp.int32, (2 * RANK, RANK), 0)
    chosen = jnp.where(spread == table_row, 1.0, 0.0).astype(BF16)
    picked = nn(candidates, chosen)
    return picked.astype(BF16), picked[0:64] + picked[64:128]


def softmax3(exponent):
    top = jnp.max(exponent, axis=0, keepdims=True)
    weights = jnp.exp2(3.0 * (exponent - top))
    return weights / jnp.sum(weights, axis=0, keepdims=True)


def kernel(
    near_list,
    far_list,
    top_far_list,
    points,
    coefficients,
    leaf_skeleton,
    node_skeleton,
    pair_skeleton,
    quad_skeleton,
    top_skeleton,
    out,
    near_points,
    near_values,
    node_points,
    node_values,
    node_lists,
    list_scalars,
    top_points,
    top_values,
    field_out,
    field_in,
    weights_t,
    leaf_left,
    near_right,
    values_high,
    values_low,
    basis_t_high,
    basis_t_low,
    basis_high,
    basis_low,
    node_right,
    upper_right,
    chain_high,
    chain_low,
    near_send,
    near_recv,
    gpts_send,
    gpts_recv,
    glist_send,
    glist_recv,
    gval_send,
    gval_recv,
    edge_send,
    edge_recv,
    tpts_send,
    tpts_recv,
    tval_send,
    tval_recv,
    back_send,
    back_recv,
    local_sem,
):
    me = lax.axis_index("leaf")
    place = lax.rem(me, GROUP)
    group = me // GROUP
    right_device = lax.rem(me + 1, DEVICES)
    left_device = lax.rem(me + DEVICES - 1, DEVICES)
    next_group = lax.rem(group + 1, TOPS) * GROUP + place
    previous_group = lax.rem(group + TOPS - 1, TOPS) * GROUP + place

    core = lax.rem(place, 2)
    sibling_place = place + 1 - 2 * core
    sibling = group * GROUP + sibling_place

    def mate(step):
        return group * GROUP + lax.rem(place + step, GROUP)

    def peer(step):
        return lax.rem(group + step, TOPS) * GROUP + place

    barrier = pltpu.get_barrier_semaphore()
    partners = [right_device, left_device]
    partners += [mate(step) for step in range(1, GROUP)]
    partners += [peer(step) for step in range(1, TOPS)]
    for partner in partners:
        pl.semaphore_signal(barrier, inc=1, device_id=(partner,), device_id_type=MESH)

    def remote(source, target, send, recv, device):
        return pltpu.make_async_remote_copy(
            src_ref=source, dst_ref=target, send_sem=send, recv_sem=recv, device_id=(device,), device_id_type=MESH
        )

    started = []

    def start(*args):
        copy = remote(*args)
        copy.start()
        started.append(copy)

    high, low, norms, ones, rest = parts(points[...] * SCALE)
    right_rows = jnp.concatenate([low, high, high, ones, norms, rest], axis=0).astype(BF16)
    leaf_picks = []
    for leaf in range(2):
        right = right_rows[:, leaf * LEAF : (leaf + 1) * LEAF]
        near_right[2 + leaf] = right
        leaf_picks.append(pick(right, leaf_skeleton[leaf : leaf + 1, :])[0])
    picks = jnp.concatenate(leaf_picks, axis=1)
    node_pick, node_pick_points = pick(picks, node_skeleton[...])
    node_points[4 + place] = node_pick_points
    lane_row = lax.broadcasted_iota(jnp.int32, (1, 128), 1)
    node_lists[place] = jnp.where(
        lane_row == 0, far_list[0, 0], jnp.where(lane_row == 1, far_list[0, 1], far_list[0, 2])
    )
    pl.semaphore_wait(barrier, len(partners))
    mine = node_points.at[4 + place]
    for step in (2, 4, 6):
        start(mine, mine, gpts_send.at[step], gpts_recv.at[step], mate(step))
    start(mine, mine, gpts_send.at[0], gpts_recv.at[0], sibling)

    transfer = split(softmax3(exponents(node_pick, picks)))
    for leaf in range(2):
        rows = slice(leaf * LEAF, (leaf + 1) * LEAF)
        half = slice(leaf * RANK, (leaf + 1) * RANK)
        basis = softmax3(exponents(leaf_picks[leaf], near_right[2 + leaf]))
        basis_t = product3(nn, (transfer[0][:, half], transfer[1][:, half]), split(basis))
        basis_t_high[:, rows], basis_t_low[:, rows] = split(basis_t)
        values_high[2 + leaf], values_low[2 + leaf] = split(coefficients[rows, :])
    weights = product3(
        nn,
        (basis_t_high[...], basis_t_low[...]),
        (values_high[2:4].reshape(2 * LEAF, RHS), values_low[2:4].reshape(2 * LEAF, RHS)),
    )
    weights_t[...] = jnp.transpose(weights).reshape(GROUP, SHARE, RANK)
    for step in range(1, GROUP):
        start(
            weights_t.at[lax.rem(place + step, GROUP)],
            node_values.at[4 + place],
            gval_send.at[step],
            gval_recv.at[step],
            mate(step),
        )
    node_values[4 + place] = weights_t[place]
    for step in range(1, GROUP):
        start(node_lists.at[place], node_lists.at[place], glist_send.at[step], glist_recv.at[step], mate(step))

    for side, device in ((0, right_device), (1, left_device)):
        start(points, near_points.at[side], near_send.at[side, 0], near_recv.at[side, 0], device)
        for part in range(4):
            rows = pl.ds(part * 256, 256)
            start(
                coefficients.at[rows, :],
                near_values.at[side, rows, :],
                near_send.at[side, part + 1],
                near_recv.at[side, part + 1],
                device,
            )

    def near_tile(leaf, half, position):
        rows = pl.ds(pl.multiple_of(leaf * LEAF + half * 256, 256), 256)
        tile = split(jnp.exp2(nn(leaf_left[rows, :], near_right[position])))
        return rows, product3(nn, tile, (values_high[position], values_low[position]))

    left_rows = jnp.concatenate([high, low, high, norms, ones, rest], axis=0)
    for leaf in range(2):
        rows = slice(leaf * LEAF, (leaf + 1) * LEAF)
        leaf_left[rows, :] = jnp.transpose(left_rows[:, rows]).astype(BF16)
        for half in range(2):
            tile_rows, value = near_tile(leaf, half, 2 + leaf)
            out[tile_rows, :] = value

    for step in (2, 4, 6):
        landed = node_points.at[4 + lax.rem(place + GROUP - step, GROUP)]
        remote(landed, landed, gpts_send.at[step], gpts_recv.at[step], sibling).wait_recv()
        start(landed, landed, gpts_send.at[1 + step], gpts_recv.at[1 + step], sibling)
    for leaf in range(2):
        rows = slice(leaf * LEAF, (leaf + 1) * LEAF)
        basis_high[rows, :] = jnp.transpose(basis_t_high[:, rows].astype(F32)).astype(BF16)
        basis_low[rows, :] = jnp.transpose(basis_t_low[:, rows].astype(F32)).astype(BF16)
    landed = node_points.at[4 + sibling_place]
    remote(landed, landed, gpts_send.at[0], gpts_recv.at[0], sibling).wait_recv()
    for step in (2, 4, 6):
        landed = node_points.at[4 + lax.rem(sibling_place + GROUP - step, GROUP)]
        remote(landed, landed, gpts_send.at[1 + step], gpts_recv.at[1 + step], sibling).wait_recv()
    for node in range(4, 12):
        node_right[node] = right_form(node_points[node])

    pair_candidates = [
        jnp.concatenate([node_right[4 + 2 * pair], node_right[5 + 2 * pair]], axis=1) for pair in range(4)
    ]
    for pair in range(4):
        upper_right[pair] = pick(pair_candidates[pair], pair_skeleton[pl.ds(group * 4 + pair, 1), :])[0]
    quad_candidates = [
        jnp.concatenate([upper_right[2 * quad], upper_right[2 * quad + 1]], axis=1) for quad in range(2)
    ]
    for quad in range(2):
        upper_right[4 + quad] = pick(quad_candidates[quad], quad_skeleton[pl.ds(group * 2 + quad, 1), :])[0]
    top_candidates = jnp.concatenate([upper_right[4], upper_right[5]], axis=1)
    top_right, top_picked = pick(top_candidates, top_skeleton[pl.ds(group, 1), :])
    upper_right[6] = top_right
    top_points[core, group] = jnp.where(core == 0, top_picked[0:32], top_picked[32:64])
    share = top_points.at[core, group]
    for step in range(1, TOPS):
        start(share, share, tpts_send.at[step], tpts_recv.at[step], peer(step))
    for side, source, target, device in ((0, 8, 0, next_group), (1, 4, 12, previous_group)):
        start(
            node_points.at[pl.ds(source + 2 * core, 2)],
            node_points.at[pl.ds(target + 2 * core, 2)],
            edge_send.at[side],
            edge_recv.at[side],
            device,
        )

    top_transfer = split(softmax3(exponents(upper_right[6], top_candidates)))
    for quad in range(2):
        half = slice(quad * RANK, (quad + 1) * RANK)
        transfer = split(softmax3(exponents(upper_right[4 + quad], quad_candidates[quad])))
        upper = split(product3(nn, (top_transfer[0][:, half], top_transfer[1][:, half]), transfer))
        for side in range(2):
            pair = 2 * quad + side
            half = slice(side * RANK, (side + 1) * RANK)
            transfer = split(softmax3(exponents(upper_right[pair], pair_candidates[pair])))
            chain = split(product3(nn, (upper[0][:, half], upper[1][:, half]), transfer))
            for child in range(2):
                columns = slice(child * RANK, (child + 1) * RANK)
                chain_high[2 * pair + child] = chain[0][:, columns]
                chain_low[2 * pair + child] = chain[1][:, columns]

    for step in range(1, GROUP):
        source = 4 + lax.rem(place + GROUP - step, GROUP)
        remote(
            weights_t.at[0], node_values.at[source], gval_send.at[step], gval_recv.at[step], mate(step)
        ).wait_recv()
    start(node_values.at[pl.ds(8, 4)], node_values.at[pl.ds(0, 4)], edge_send.at[2], edge_recv.at[2], next_group)
    start(node_values.at[pl.ds(4, 4)], node_values.at[pl.ds(12, 4)], edge_send.at[3], edge_recv.at[3], previous_group)
    total = jnp.zeros((SHARE, RANK), F32)
    for node in range(GROUP):
        total = total + thin_product(nt, node_values[4 + node], (chain_high[node], chain_low[node]))
    top_values[group] = total
    for step in range(1, TOPS):
        start(top_values.at[group], top_values.at[group], tval_send.at[step], tval_recv.at[step], peer(step))

    for side, target in ((0, 0), (1, 12)):
        landed = node_points.at[pl.ds(target + 2 * core, 2)]
        remote(landed, landed, edge_send.at[side], edge_recv.at[side], sibling).wait_recv()
        start(landed, landed, edge_send.at[4 + side], edge_recv.at[4 + side], sibling)
    for step in range(1, GROUP):
        source = lax.rem(place + GROUP - step, GROUP)
        remote(
            node_lists.at[source], node_lists.at[source], glist_send.at[step], glist_recv.at[step], mate(step)
        ).wait_recv()
    to_scalars = pltpu.make_async_copy(node_lists, list_scalars, local_sem)
    to_scalars.start()
    to_scalars.wait()
    for side, target in ((0, 0), (1, 12)):
        landed = node_points.at[pl.ds(target + 2 - 2 * core, 2)]
        remote(landed, landed, edge_send.at[4 + side], edge_recv.at[4 + side], sibling).wait_recv()
    for node in (0, 1, 2, 3, 12, 13, 14, 15):
        node_right[node] = right_form(node_points[node])
    for side, target in ((0, 0), (1, 12)):
        landed = node_values.at[pl.ds(target, 4)]
        remote(landed, landed, edge_send.at[2 + side], edge_recv.at[2 + side], sibling).wait_recv()

    def far_node(node, carry):
        mine_right = node_right[4 + node]
        total = jnp.zeros((SHARE, RANK), F32)
        for slot in range(FAR1):
            entry = list_scalars[node, 0, slot]
            weight = (jnp.minimum(entry, 0) + 1).astype(F32)
            position = jnp.maximum(entry - group * GROUP + 4, 0)
            tile = split(jnp.exp2(exponents(node_right[position], mine_right)))
            total = total + weight * thin_product(nn, node_values[position], tile)
        field_out[node] = total
        return carry

    lax.fori_loop(0, GROUP // 2, far_node, 0, unroll=2)
    for step in range(1, TOPS):
        landed = top_points.at[core, lax.rem(group + TOPS - step, TOPS)]
        remote(landed, landed, tpts_send.at[step], tpts_recv.at[step], sibling).wait_recv()
    start(top_points.at[core], top_points.at[core], tpts_send.at[0], tpts_recv.at[0], sibling)
    lax.fori_loop(GROUP // 2, GROUP, far_node, 0, unroll=2)

    landed = top_points.at[1 - core]
    remote(landed, landed, tpts_send.at[0], tpts_recv.at[0], sibling).wait_recv()
    tiles = []
    for slot in range(FAR4):
        source = top_far_list[slot, group]
        tiles.append(split(jnp.exp2(exponents(right_form(top_points[:, source].reshape(FEAT, RANK)), upper_right[6]))))
    for step in range(1, TOPS):
        source = lax.rem(group + TOPS - step, TOPS)
        remote(
            top_values.at[source], top_values.at[source], tval_send.at[step], tval_recv.at[step], peer(step)
        ).wait_recv()
    top_field = jnp.zeros((SHARE, RANK), F32)
    for slot in range(FAR4):
        source = top_far_list[slot, group]
        top_field = top_field + thin_product(nn, top_values[source], tiles[slot])
    for node in range(GROUP):
        field_out[node] = field_out[node] + thin_product(nn, top_field, (chain_high[node], chain_low[node]))
    for step in range(1, GROUP):
        start(
            field_out.at[lax.rem(place + step, GROUP)],
            field_in.at[place],
            back_send.at[step],
            back_recv.at[step],
            mate(step),
        )
    field_in[place] = field_out[place]

    for side in range(2):
        for part in range(5):
            if part == 0:
                landed = near_points.at[side]
            else:
                landed = near_values.at[side, pl.ds((part - 1) * 256, 256), :]
            remote(landed, landed, near_send.at[side, part], near_recv.at[side, part], right_device).wait_recv()
        for leaf in range(2):
            slot = 4 * side + leaf
            rows = slice(leaf * LEAF, (leaf + 1) * LEAF)
            near_right[slot] = right_form(near_points[side, :, rows] * SCALE)
            values_high[slot], values_low[slot] = split(near_values[side, rows, :])

    def other_tile(step, carry):
        leaf = step // 2
        entry = near_list[leaf, 1 + step % 2]
        position = jnp.maximum(entry - 2 * me + 2, 0)
        weight = (jnp.minimum(entry, 0) + 1).astype(F32)
        for half in range(2):
            rows, value = near_tile(leaf, half, position)
            out[rows, :] = out[rows, :] + weight * value
        return carry

    lax.fori_loop(0, 4, other_tile, 0)

    for step in range(1, GROUP):
        source = lax.rem(place + GROUP - step, GROUP)
        remote(
            field_out.at[0], field_in.at[source], back_send.at[step], back_recv.at[step], mate(step)
        ).wait_recv()
    field = split(jnp.transpose(field_in[...].reshape(RHS, RANK)))
    for quarter in range(4):
        rows = slice(quarter * 256, (quarter + 1) * 256)
        out[rows, :] = out[rows, :] + product3(nn, (basis_high[rows, :], basis_low[rows, :]), field)
    for copy in started:
        copy.wait_send()


def body(
    points,
    coefficients,
    leaf_skeleton,
    node_skeleton,
    pair_skeleton,
    quad_skeleton,
    top_skeleton,
    near_list,
    far_list,
    top_far_list,
):
    vmem = pl.BlockSpec(memory_space=pltpu.VMEM)
    smem = pl.BlockSpec(memory_space=pltpu.SMEM)
    dma = pltpu.SemaphoreType.DMA
    return pl.pallas_call(
        kernel,
        out_shape=jax.ShapeDtypeStruct((2 * LEAF, RHS), F32),
        in_specs=[smem] * 3 + [vmem] * 7,
        out_specs=vmem,
        scratch_shapes=[
            pltpu.VMEM((2, FEAT, 2 * LEAF), F32),
            pltpu.VMEM((2, 2 * LEAF, RHS), F32),
            pltpu.VMEM((16, FEAT, RANK), F32),
            pltpu.VMEM((16, SHARE, RANK), F32),
            pltpu.VMEM((GROUP, 1, 128), jnp.int32),
            pltpu.SMEM((GROUP, 1, 128), jnp.int32),
            pltpu.VMEM((2, TOPS, FEAT // 2, RANK), F32),
            pltpu.VMEM((TOPS, SHARE, RANK), F32),
            pltpu.VMEM((GROUP, SHARE, RANK), F32),
            pltpu.VMEM((GROUP, SHARE, RANK), F32),
            pltpu.VMEM((GROUP, SHARE, RANK), F32),
            pltpu.VMEM((2 * LEAF, 256), BF16),
            pltpu.VMEM((6, 256, LEAF), BF16),
            pltpu.VMEM((6, LEAF, RHS), BF16),
            pltpu.VMEM((6, LEAF, RHS), BF16),
            pltpu.VMEM((RANK, 2 * LEAF), BF16),
            pltpu.VMEM((RANK, 2 * LEAF), BF16),
            pltpu.VMEM((2 * LEAF, RANK), BF16),
            pltpu.VMEM((2 * LEAF, RANK), BF16),
            pltpu.VMEM((16, 256, RANK), BF16),
            pltpu.VMEM((7, 256, RANK), BF16),
            pltpu.VMEM((GROUP, RANK, RANK), BF16),
            pltpu.VMEM((GROUP, RANK, RANK), BF16),
            dma((2, 5)),
            dma((2, 5)),
            dma((GROUP,)),
            dma((GROUP,)),
            dma((GROUP,)),
            dma((GROUP,)),
            dma((GROUP,)),
            dma((GROUP,)),
            dma((6,)),
            dma((6,)),
            dma((TOPS,)),
            dma((TOPS,)),
            dma((TOPS,)),
            dma((TOPS,)),
            dma((GROUP,)),
            dma((GROUP,)),
            dma,
        ],
        compiler_params=pltpu.CompilerParams(
            collective_id=0, has_side_effects=True, vmem_limit_bytes=56 * 1024 * 1024
        ),
    )(
        near_list,
        far_list,
        top_far_list.T,
        points.T,
        coefficients,
        leaf_skeleton,
        node_skeleton,
        pair_skeleton,
        quad_skeleton,
        top_skeleton,
    )


def solution(mesh):
    return jax.shard_map(
        body,
        mesh=mesh,
        in_specs=(
            P("leaf", None),
            P("leaf", None),
            P("leaf", None),
            P("leaf", None),
            P(),
            P(),
            P(),
            P("leaf", None),
            P("leaf", None),
            P(),
        ),
        out_specs=P("leaf", None),
        check_vma=False,
    )
```

```python
import math

import jax
import jax.numpy as jnp
from jax import lax
from jax.experimental import pallas as pl
from jax.experimental.pallas import tpu as pltpu
from jax.sharding import PartitionSpec as P

FEAT = 64
RHS = 256
RANK = 256
LEAF = 512
NEAR = 3
FAR1 = 3
FAR4 = 3
GROUP = 8
TOPS = 16
SHARE = RHS // GROUP
HALF = RANK // 2

MESH = pl.DeviceIdType.MESH
F32 = jnp.float32
BF16 = jnp.bfloat16
SCALE = math.sqrt(2.0 * math.log2(math.e) / FEAT)


def dot(left, right, dims):
    return lax.dot_general(left, right, (dims, ((), ())), preferred_element_type=F32)


def nn(left, right):
    return dot(left, right, ((1,), (0,)))


def nt(left, right):
    return dot(left, right, ((1,), (1,)))


def tn(left, right):
    return dot(left, right, ((0,), (0,)))


def split(values):
    high = values.astype(BF16)
    low = (values - high.astype(F32)).astype(BF16)
    return high, low


def product3(mul, left, right):
    return mul(left[0], right[0]) + (mul(left[0], right[1]) + mul(left[1], right[0]))


def thin_product(mul, left, right):
    rows = left.shape[0]
    high, low = split(left)
    both = mul(jnp.concatenate([high, low], axis=0), right[0])
    return both[:rows] + (both[rows:] + mul(high, right[1]))


def parts(points):
    high = points.astype(BF16).astype(F32)
    low = points - high
    norm = -0.5 * jnp.sum(points * points, axis=0, keepdims=True)
    norm1 = norm.astype(BF16).astype(F32)
    norm2 = (norm - norm1).astype(BF16).astype(F32)
    norm3 = norm - norm1 - norm2
    row = lax.broadcasted_iota(jnp.int32, (16, points.shape[1]), 0)
    norms = jnp.where(row == 0, norm1, jnp.where(row == 1, norm2, jnp.where(row == 2, norm3, 0.0)))
    ones = jnp.where(row < 3, 1.0, 0.0)
    rest = jnp.zeros((32, points.shape[1]), F32)
    return high, low, norms, ones, rest


def right_form(points):
    high, low, norms, ones, rest = parts(points)
    return jnp.concatenate([low, high, high, ones, norms, rest], axis=0).astype(BF16)


def left_of(right):
    return jnp.concatenate(
        [right[64:128], right[0:64], right[128:192], right[208:224], right[192:208], right[224:256]], axis=0
    )


def exponents(left_points, right_points):
    return tn(left_of(left_points), right_points)


def pick(candidates, table_row):
    spread = lax.broadcasted_iota(jnp.int32, (2 * RANK, RANK), 0)
    chosen = jnp.where(spread == table_row, 1.0, 0.0).astype(BF16)
    picked = nn(candidates, chosen)
    return picked.astype(BF16), picked[0:64] + picked[64:128]


def softmax3(exponent):
    top = jnp.max(exponent, axis=0, keepdims=True)
    weights = jnp.exp2(3.0 * (exponent - top))
    return weights / jnp.sum(weights, axis=0, keepdims=True)


def kernel(
    near_list,
    far_list,
    top_far_list,
    points,
    coefficients,
    leaf_skeleton,
    node_skeleton,
    pair_skeleton,
    quad_skeleton,
    top_skeleton,
    out,
    near_points,
    near_values,
    node_points,
    node_values,
    node_lists,
    list_scalars,
    top_points,
    top_values,
    field_out,
    field_in,
    weights_t,
    leaf_left,
    near_right,
    values_high,
    values_low,
    basis_t_high,
    basis_t_low,
    basis_high,
    basis_low,
    node_right,
    upper_right,
    chain_high,
    chain_low,
    near_send,
    near_recv,
    relay_send,
    gpts_send,
    gpts_recv,
    glist_send,
    glist_recv,
    gval_send,
    gval_recv,
    edge_send,
    edge_recv,
    tpts_send,
    tpts_recv,
    tval_send,
    tval_recv,
    back_send,
    back_recv,
    local_sem,
):
    me = lax.axis_index("leaf")
    place = lax.rem(me, GROUP)
    group = me // GROUP
    next_group = lax.rem(group + 1, TOPS) * GROUP + place
    previous_group = lax.rem(group + TOPS - 1, TOPS) * GROUP + place

    core = lax.rem(place, 2)
    sibling_place = place + 1 - 2 * core
    sibling = group * GROUP + sibling_place

    def mate(step):
        return group * GROUP + lax.rem(place + step, GROUP)

    def peer(step):
        return lax.rem(group + step, TOPS) * GROUP + place

    barrier = pltpu.get_barrier_semaphore()
    partners = [mate(step) for step in range(1, GROUP)]
    partners += [peer(step) for step in range(1, TOPS)]
    for partner in partners:
        pl.semaphore_signal(barrier, inc=1, device_id=(partner,), device_id_type=MESH)

    def remote(source, target, send, recv, device):
        return pltpu.make_async_remote_copy(
            src_ref=source, dst_ref=target, send_sem=send, recv_sem=recv, device_id=(device,), device_id_type=MESH
        )

    started = []

    def start(*args):
        copy = remote(*args)
        copy.start()
        started.append(copy)

    high, low, norms, ones, rest = parts(points[...] * SCALE)
    right_rows = jnp.concatenate([low, high, high, ones, norms, rest], axis=0).astype(BF16)
    leaf_picks = []
    for leaf in range(2):
        right = right_rows[:, leaf * LEAF : (leaf + 1) * LEAF]
        near_right[2 + leaf] = right
        leaf_picks.append(pick(right, leaf_skeleton[leaf : leaf + 1, :])[0])
    picks = jnp.concatenate(leaf_picks, axis=1)
    node_pick, node_pick_points = pick(picks, node_skeleton[...])
    node_points[4 + place] = node_pick_points
    lane_row = lax.broadcasted_iota(jnp.int32, (1, 128), 1)
    node_lists[place] = jnp.where(
        lane_row == 0, far_list[0, 0], jnp.where(lane_row == 1, far_list[0, 1], far_list[0, 2])
    )
    pl.semaphore_wait(barrier, len(partners))
    mine = node_points.at[4 + place]
    for step in (2, 4, 6):
        start(mine, mine, gpts_send.at[step], gpts_recv.at[step], mate(step))
    start(mine, mine, gpts_send.at[0], gpts_recv.at[0], sibling)

    transfer = split(softmax3(exponents(node_pick, picks)))
    for leaf in range(2):
        rows = slice(leaf * LEAF, (leaf + 1) * LEAF)
        half = slice(leaf * RANK, (leaf + 1) * RANK)
        basis = softmax3(exponents(leaf_picks[leaf], near_right[2 + leaf]))
        basis_t = product3(nn, (transfer[0][:, half], transfer[1][:, half]), split(basis))
        basis_t_high[:, rows], basis_t_low[:, rows] = split(basis_t)
        values_high[2 + leaf], values_low[2 + leaf] = split(coefficients[rows, :])
    weights = product3(
        nn,
        (basis_t_high[...], basis_t_low[...]),
        (values_high[2:4].reshape(2 * LEAF, RHS), values_low[2:4].reshape(2 * LEAF, RHS)),
    )
    weights_t[...] = jnp.transpose(weights).reshape(GROUP, SHARE, RANK)
    for step in range(1, GROUP):
        start(
            weights_t.at[lax.rem(place + step, GROUP)],
            node_values.at[4 + place],
            gval_send.at[step],
            gval_recv.at[step],
            mate(step),
        )
    node_values[4 + place] = weights_t[place]
    for step in range(1, GROUP):
        start(node_lists.at[place], node_lists.at[place], glist_send.at[step], glist_recv.at[step], mate(step))

    def near_refs(slot, half):
        columns = pl.ds(half * LEAF, LEAF)
        return near_points.at[slot, :, columns], near_values.at[slot, columns, :]

    def relay(slot, half, target, device):
        for kind, landed in enumerate(near_refs(slot, half)):
            part = 2 * half + kind
            send = relay_send.at[target, kind]
            yield (
                (landed, landed, send, near_recv.at[slot, part], device),
                (landed, near_refs(target, half)[kind], send, near_recv.at[target, part], device),
            )

    def relays():
        at_end = [relay(2, 0, 0, mate(1)), relay(3, 1, 1, previous_group)]
        at_start = [relay(2, 1, 0, next_group), relay(3, 0, 1, mate(GROUP - 1))]
        return ((place == GROUP - 1, at_end), (place == 0, at_start))

    last = place // (GROUP - 1)
    first = (GROUP - 1 - place) // (GROUP - 1)
    for half in range(2):
        columns = pl.ds(half * LEAF, LEAF)
        for side, edge, inner, outer in ((0, last, mate(1), next_group), (1, first, mate(GROUP - 1), previous_group)):
            slot = side + 2 * edge
            device = (1 - edge) * inner + edge * (outer if half == 0 else inner)
            for kind, source in enumerate((points.at[:, columns], coefficients.at[columns, :])):
                part = 2 * half + kind
                start(
                    source, near_refs(slot, half)[kind], near_send.at[side, part], near_recv.at[slot, part], device
                )

    def near_tile(leaf, half, position):
        rows = pl.ds(pl.multiple_of(leaf * LEAF + half * 256, 256), 256)
        tile = split(jnp.exp2(nn(leaf_left[rows, :], near_right[position])))
        return rows, product3(nn, tile, (values_high[position], values_low[position]))

    left_rows = jnp.concatenate([high, low, high, norms, ones, rest], axis=0)
    for leaf in range(2):
        rows = slice(leaf * LEAF, (leaf + 1) * LEAF)
        leaf_left[rows, :] = jnp.transpose(left_rows[:, rows]).astype(BF16)
        for half in range(2):
            tile_rows, value = near_tile(leaf, half, 2 + leaf)
            out[tile_rows, :] = value

    for step in (2, 4, 6):
        landed = node_points.at[4 + lax.rem(place + GROUP - step, GROUP)]
        remote(landed, landed, gpts_send.at[step], gpts_recv.at[step], sibling).wait_recv()
        start(landed, landed, gpts_send.at[1 + step], gpts_recv.at[1 + step], sibling)
    for leaf in range(2):
        rows = slice(leaf * LEAF, (leaf + 1) * LEAF)
        basis_high[rows, :] = jnp.transpose(basis_t_high[:, rows].astype(F32)).astype(BF16)
        basis_low[rows, :] = jnp.transpose(basis_t_low[:, rows].astype(F32)).astype(BF16)
    landed = node_points.at[4 + sibling_place]
    remote(landed, landed, gpts_send.at[0], gpts_recv.at[0], sibling).wait_recv()
    for step in (2, 4, 6):
        landed = node_points.at[4 + lax.rem(sibling_place + GROUP - step, GROUP)]
        remote(landed, landed, gpts_send.at[1 + step], gpts_recv.at[1 + step], sibling).wait_recv()
    for node in range(4, 12):
        node_right[node] = right_form(node_points[node])

    pair_candidates = [
        jnp.concatenate([node_right[4 + 2 * pair], node_right[5 + 2 * pair]], axis=1) for pair in range(4)
    ]
    for pair in range(4):
        upper_right[pair] = pick(pair_candidates[pair], pair_skeleton[pl.ds(group * 4 + pair, 1), :])[0]
    quad_candidates = [
        jnp.concatenate([upper_right[2 * quad], upper_right[2 * quad + 1]], axis=1) for quad in range(2)
    ]
    for quad in range(2):
        upper_right[4 + quad] = pick(quad_candidates[quad], quad_skeleton[pl.ds(group * 2 + quad, 1), :])[0]
    top_candidates = jnp.concatenate([upper_right[4], upper_right[5]], axis=1)
    top_right, top_picked = pick(top_candidates, top_skeleton[pl.ds(group, 1), :])
    upper_right[6] = top_right
    top_points[core, group] = jnp.where(core == 0, top_picked[0:32], top_picked[32:64])
    share = top_points.at[core, group]
    for step in range(1, TOPS):
        start(share, share, tpts_send.at[step], tpts_recv.at[step], peer(step))
    for side, source, target, device in ((0, 8, 0, next_group), (1, 4, 12, previous_group)):
        start(
            node_points.at[pl.ds(source + 2 * core, 2)],
            node_points.at[pl.ds(target + 2 * core, 2)],
            edge_send.at[side],
            edge_recv.at[side],
            device,
        )

    top_transfer = split(softmax3(exponents(upper_right[6], top_candidates)))
    for quad in range(2):
        half = slice(quad * RANK, (quad + 1) * RANK)
        transfer = split(softmax3(exponents(upper_right[4 + quad], quad_candidates[quad])))
        upper = split(product3(nn, (top_transfer[0][:, half], top_transfer[1][:, half]), transfer))
        for side in range(2):
            pair = 2 * quad + side
            half = slice(side * RANK, (side + 1) * RANK)
            transfer = split(softmax3(exponents(upper_right[pair], pair_candidates[pair])))
            chain = split(product3(nn, (upper[0][:, half], upper[1][:, half]), transfer))
            for child in range(2):
                columns = slice(child * RANK, (child + 1) * RANK)
                chain_high[2 * pair + child] = chain[0][:, columns]
                chain_low[2 * pair + child] = chain[1][:, columns]

    for step in range(1, GROUP):
        source = 4 + lax.rem(place + GROUP - step, GROUP)
        remote(
            weights_t.at[0], node_values.at[source], gval_send.at[step], gval_recv.at[step], mate(step)
        ).wait_recv()
    start(node_values.at[pl.ds(8, 4)], node_values.at[pl.ds(0, 4)], edge_send.at[2], edge_recv.at[2], next_group)
    start(node_values.at[pl.ds(4, 4)], node_values.at[pl.ds(12, 4)], edge_send.at[3], edge_recv.at[3], previous_group)
    total = jnp.zeros((SHARE, RANK), F32)
    for node in range(GROUP):
        total = total + thin_product(nt, node_values[4 + node], (chain_high[node], chain_low[node]))
    top_values[group] = total
    for step in range(1, TOPS):
        start(top_values.at[group], top_values.at[group], tval_send.at[step], tval_recv.at[step], peer(step))

    for here, paths in relays():

        @pl.when(here)
        def _():
            for path in paths:
                for arrived, copy in path:
                    remote(*arrived).wait_recv()
                    remote(*copy).start()

    for side, target in ((0, 0), (1, 12)):
        landed = node_points.at[pl.ds(target + 2 * core, 2)]
        remote(landed, landed, edge_send.at[side], edge_recv.at[side], sibling).wait_recv()
        start(landed, landed, edge_send.at[4 + side], edge_recv.at[4 + side], sibling)
    for step in range(1, GROUP):
        source = lax.rem(place + GROUP - step, GROUP)
        remote(
            node_lists.at[source], node_lists.at[source], glist_send.at[step], glist_recv.at[step], mate(step)
        ).wait_recv()
    to_scalars = pltpu.make_async_copy(node_lists, list_scalars, local_sem)
    to_scalars.start()
    to_scalars.wait()
    for side, target in ((0, 0), (1, 12)):
        landed = node_points.at[pl.ds(target + 2 - 2 * core, 2)]
        remote(landed, landed, edge_send.at[4 + side], edge_recv.at[4 + side], sibling).wait_recv()
    for node in (0, 1, 2, 3, 12, 13, 14, 15):
        node_right[node] = right_form(node_points[node])
    for side, target in ((0, 0), (1, 12)):
        landed = node_values.at[pl.ds(target, 4)]
        remote(landed, landed, edge_send.at[2 + side], edge_recv.at[2 + side], sibling).wait_recv()

    def far_node(node, carry):
        mine_right = node_right[4 + node]
        total = jnp.zeros((SHARE, RANK), F32)
        for slot in range(FAR1):
            entry = list_scalars[node, 0, slot]
            weight = (jnp.minimum(entry, 0) + 1).astype(F32)
            position = jnp.maximum(entry - group * GROUP + 4, 0)
            tile = split(jnp.exp2(exponents(node_right[position], mine_right)))
            total = total + weight * thin_product(nn, node_values[position], tile)
        field_out[node] = total
        return carry

    lax.fori_loop(0, GROUP // 2, far_node, 0, unroll=2)
    for step in range(1, TOPS):
        landed = top_points.at[core, lax.rem(group + TOPS - step, TOPS)]
        remote(landed, landed, tpts_send.at[step], tpts_recv.at[step], sibling).wait_recv()
    start(top_points.at[core], top_points.at[core], tpts_send.at[0], tpts_recv.at[0], sibling)
    lax.fori_loop(GROUP // 2, GROUP, far_node, 0, unroll=2)

    landed = top_points.at[1 - core]
    remote(landed, landed, tpts_send.at[0], tpts_recv.at[0], sibling).wait_recv()
    tiles = []
    for slot in range(FAR4):
        source = top_far_list[slot, group]
        tiles.append(split(jnp.exp2(exponents(right_form(top_points[:, source].reshape(FEAT, RANK)), upper_right[6]))))
    for step in range(1, TOPS):
        source = lax.rem(group + TOPS - step, TOPS)
        remote(
            top_values.at[source], top_values.at[source], tval_send.at[step], tval_recv.at[step], peer(step)
        ).wait_recv()
    top_field = jnp.zeros((SHARE, RANK), F32)
    for slot in range(FAR4):
        source = top_far_list[slot, group]
        top_field = top_field + thin_product(nn, top_values[source], tiles[slot])
    for node in range(GROUP):
        field_out[node] = field_out[node] + thin_product(nn, top_field, (chain_high[node], chain_low[node]))
    for step in range(1, GROUP):
        start(
            field_out.at[lax.rem(place + step, GROUP)],
            field_in.at[place],
            back_send.at[step],
            back_recv.at[step],
            mate(step),
        )
    field_in[place] = field_out[place]

    for side in range(2):
        for half in range(2):
            for kind, landed in enumerate(near_refs(side, half)):
                part = 2 * half + kind
                remote(landed, landed, near_send.at[side, part], near_recv.at[side, part], sibling).wait_recv()
        for leaf in range(2):
            slot = 4 * side + leaf
            rows = slice(leaf * LEAF, (leaf + 1) * LEAF)
            near_right[slot] = right_form(near_points[side, :, rows] * SCALE)
            values_high[slot], values_low[slot] = split(near_values[side, rows, :])

    def other_tile(step, carry):
        leaf = step // 2
        entry = near_list[leaf, 1 + step % 2]
        position = jnp.maximum(entry - 2 * me + 2, 0)
        weight = (jnp.minimum(entry, 0) + 1).astype(F32)
        for half in range(2):
            rows, value = near_tile(leaf, half, position)
            out[rows, :] = out[rows, :] + weight * value
        return carry

    lax.fori_loop(0, 4, other_tile, 0)

    for step in range(1, GROUP):
        source = lax.rem(place + GROUP - step, GROUP)
        remote(
            field_out.at[0], field_in.at[source], back_send.at[step], back_recv.at[step], mate(step)
        ).wait_recv()
    field = split(jnp.transpose(field_in[...].reshape(RHS, RANK)))
    for quarter in range(4):
        rows = slice(quarter * 256, (quarter + 1) * 256)
        out[rows, :] = out[rows, :] + product3(nn, (basis_high[rows, :], basis_low[rows, :]), field)
    for copy in started:
        copy.wait_send()
    for here, paths in relays():

        @pl.when(here)
        def _():
            for path in paths:
                for _, copy in path:
                    remote(*copy).wait_send()


def body(
    points,
    coefficients,
    leaf_skeleton,
    node_skeleton,
    pair_skeleton,
    quad_skeleton,
    top_skeleton,
    near_list,
    far_list,
    top_far_list,
):
    vmem = pl.BlockSpec(memory_space=pltpu.VMEM)
    smem = pl.BlockSpec(memory_space=pltpu.SMEM)
    dma = pltpu.SemaphoreType.DMA
    return pl.pallas_call(
        kernel,
        out_shape=jax.ShapeDtypeStruct((2 * LEAF, RHS), F32),
        in_specs=[smem] * 3 + [vmem] * 7,
        out_specs=vmem,
        scratch_shapes=[
            pltpu.VMEM((4, FEAT, 2 * LEAF), F32),
            pltpu.VMEM((4, 2 * LEAF, RHS), F32),
            pltpu.VMEM((16, FEAT, RANK), F32),
            pltpu.VMEM((16, SHARE, RANK), F32),
            pltpu.VMEM((GROUP, 1, 128), jnp.int32),
            pltpu.SMEM((GROUP, 1, 128), jnp.int32),
            pltpu.VMEM((2, TOPS, FEAT // 2, RANK), F32),
            pltpu.VMEM((TOPS, SHARE, RANK), F32),
            pltpu.VMEM((GROUP, SHARE, RANK), F32),
            pltpu.VMEM((GROUP, SHARE, RANK), F32),
            pltpu.VMEM((GROUP, SHARE, RANK), F32),
            pltpu.VMEM((2 * LEAF, 256), BF16),
            pltpu.VMEM((6, 256, LEAF), BF16),
            pltpu.VMEM((6, LEAF, RHS), BF16),
            pltpu.VMEM((6, LEAF, RHS), BF16),
            pltpu.VMEM((RANK, 2 * LEAF), BF16),
            pltpu.VMEM((RANK, 2 * LEAF), BF16),
            pltpu.VMEM((2 * LEAF, RANK), BF16),
            pltpu.VMEM((2 * LEAF, RANK), BF16),
            pltpu.VMEM((16, 256, RANK), BF16),
            pltpu.VMEM((7, 256, RANK), BF16),
            pltpu.VMEM((GROUP, RANK, RANK), BF16),
            pltpu.VMEM((GROUP, RANK, RANK), BF16),
            dma((2, 4)),
            dma((4, 4)),
            dma((2, 2)),
            dma((GROUP,)),
            dma((GROUP,)),
            dma((GROUP,)),
            dma((GROUP,)),
            dma((GROUP,)),
            dma((GROUP,)),
            dma((6,)),
            dma((6,)),
            dma((TOPS,)),
            dma((TOPS,)),
            dma((TOPS,)),
            dma((TOPS,)),
            dma((GROUP,)),
            dma((GROUP,)),
            dma,
        ],
        compiler_params=pltpu.CompilerParams(
            collective_id=0, has_side_effects=True, vmem_limit_bytes=56 * 1024 * 1024
        ),
    )(
        near_list,
        far_list,
        top_far_list.T,
        points.T,
        coefficients,
        leaf_skeleton,
        node_skeleton,
        pair_skeleton,
        quad_skeleton,
        top_skeleton,
    )


def solution(mesh):
    return jax.shard_map(
        body,
        mesh=mesh,
        in_specs=(
            P("leaf", None),
            P("leaf", None),
            P("leaf", None),
            P("leaf", None),
            P(),
            P(),
            P(),
            P("leaf", None),
            P("leaf", None),
            P(),
        ),
        out_specs=P("leaf", None),
        check_vma=False,
    )
```

```python
import math

import jax
import jax.numpy as jnp
from jax import lax
from jax.experimental import pallas as pl
from jax.experimental.pallas import tpu as pltpu
from jax.sharding import PartitionSpec as P

FEAT = 64
RHS = 256
RANK = 256
LEAF = 512
NEAR = 3
FAR1 = 3
FAR4 = 3
GROUP = 8
TOPS = 16
SHARE = RHS // GROUP
HALF = RANK // 2

MESH = pl.DeviceIdType.MESH
F32 = jnp.float32
BF16 = jnp.bfloat16
SCALE = math.sqrt(2.0 * math.log2(math.e) / FEAT)


def dot(left, right, dims):
    return lax.dot_general(left, right, (dims, ((), ())), preferred_element_type=F32)


def nn(left, right):
    return dot(left, right, ((1,), (0,)))


def nt(left, right):
    return dot(left, right, ((1,), (1,)))


def tn(left, right):
    return dot(left, right, ((0,), (0,)))


def split(values):
    high = values.astype(BF16)
    low = (values - high.astype(F32)).astype(BF16)
    return high, low


def product3(mul, left, right):
    return mul(left[0], right[0]) + (mul(left[0], right[1]) + mul(left[1], right[0]))


def thin_product(mul, left, right):
    rows = left.shape[0]
    high, low = split(left)
    both = mul(jnp.concatenate([high, low], axis=0), right[0])
    return both[:rows] + (both[rows:] + mul(high, right[1]))


def parts(points):
    high = points.astype(BF16).astype(F32)
    low = points - high
    norm = -0.5 * jnp.sum(points * points, axis=0, keepdims=True)
    norm1 = norm.astype(BF16).astype(F32)
    norm2 = (norm - norm1).astype(BF16).astype(F32)
    norm3 = norm - norm1 - norm2
    row = lax.broadcasted_iota(jnp.int32, (16, points.shape[1]), 0)
    norms = jnp.where(row == 0, norm1, jnp.where(row == 1, norm2, jnp.where(row == 2, norm3, 0.0)))
    ones = jnp.where(row < 3, 1.0, 0.0)
    rest = jnp.zeros((32, points.shape[1]), F32)
    return high, low, norms, ones, rest


def right_form(points):
    high, low, norms, ones, rest = parts(points)
    return jnp.concatenate([low, high, high, ones, norms, rest], axis=0).astype(BF16)


def left_of(right):
    return jnp.concatenate(
        [right[64:128], right[0:64], right[128:192], right[208:224], right[192:208], right[224:256]], axis=0
    )


def exponents(left_points, right_points):
    return tn(left_of(left_points), right_points)


def pick(candidates, table_row):
    spread = lax.broadcasted_iota(jnp.int32, (2 * RANK, RANK), 0)
    chosen = jnp.where(spread == table_row, 1.0, 0.0).astype(BF16)
    picked = nn(candidates, chosen)
    return picked.astype(BF16), picked[0:64] + picked[64:128]


def softmax3(exponent):
    top = jnp.max(exponent, axis=0, keepdims=True)
    weights = jnp.exp2(3.0 * (exponent - top))
    return weights / jnp.sum(weights, axis=0, keepdims=True)


def kernel(
    near_list,
    far_list,
    top_far_list,
    points,
    coefficients,
    leaf_skeleton,
    node_skeleton,
    pair_skeleton,
    quad_skeleton,
    top_skeleton,
    out,
    near_points,
    near_values,
    node_points,
    node_values,
    node_lists,
    list_scalars,
    top_points,
    top_values,
    top_share,
    top_out,
    top_in,
    top_high,
    top_low,
    field_out,
    field_in,
    weights_t,
    leaf_left,
    near_right,
    values_high,
    values_low,
    basis_t_high,
    basis_t_low,
    basis_high,
    basis_low,
    node_right,
    upper_right,
    chain_high,
    chain_low,
    near_send,
    near_recv,
    relay_send,
    gpts_send,
    gpts_recv,
    glist_send,
    glist_recv,
    gval_send,
    gval_recv,
    edge_send,
    edge_recv,
    tpts_send,
    tpts_recv,
    tval_send,
    tval_recv,
    tout_send,
    tout_recv,
    back_send,
    back_recv,
    local_sem,
):
    me = lax.axis_index("leaf")
    place = lax.rem(me, GROUP)
    group = me // GROUP
    next_group = lax.rem(group + 1, TOPS) * GROUP + place
    previous_group = lax.rem(group + TOPS - 1, TOPS) * GROUP + place

    core = lax.rem(place, 2)
    sibling_place = place + 1 - 2 * core
    sibling = group * GROUP + sibling_place

    def mate(step):
        return group * GROUP + lax.rem(place + step, GROUP)

    quarter = lax.rem(group, 4)
    ring_first = group - quarter

    def ring(step):
        return (ring_first + lax.rem(quarter + step, 4)) * GROUP + place

    def peer(step):
        return lax.rem(group + step, TOPS) * GROUP + place

    barrier = pltpu.get_barrier_semaphore()
    partners = [mate(step) for step in range(1, GROUP)]
    partners += [peer(step) for step in range(1, TOPS)]
    for partner in partners:
        pl.semaphore_signal(barrier, inc=1, device_id=(partner,), device_id_type=MESH)

    def remote(source, target, send, recv, device):
        return pltpu.make_async_remote_copy(
            src_ref=source, dst_ref=target, send_sem=send, recv_sem=recv, device_id=(device,), device_id_type=MESH
        )

    started = []

    def start(*args):
        copy = remote(*args)
        copy.start()
        started.append(copy)

    def near_refs(slot, half):
        columns = pl.ds(half * LEAF, LEAF)
        return near_points.at[slot, :, columns], near_values.at[slot, columns, :]

    def relay(slot, half, target, device):
        for kind, landed in enumerate(near_refs(slot, half)):
            part = 2 * half + kind
            send = relay_send.at[target, kind]
            yield (
                (landed, landed, send, near_recv.at[slot, part], device),
                (landed, near_refs(target, half)[kind], send, near_recv.at[target, part], device),
            )

    def relays(half):
        if half == 0:
            at_end, at_start = relay(2, 0, 0, mate(1)), relay(3, 0, 1, mate(GROUP - 1))
        else:
            at_end, at_start = relay(3, 1, 1, previous_group), relay(2, 1, 0, next_group)
        return ((place == GROUP - 1, at_end), (place == 0, at_start))

    def pass_on(half):
        for here, path in relays(half):

            @pl.when(here)
            def _():
                for arrived, copy in path:
                    remote(*arrived).wait_recv()
                    remote(*copy).start()

    last = place // (GROUP - 1)
    first = (GROUP - 1 - place) // (GROUP - 1)
    def near_sends(half, at_edge):
        columns = pl.ds(half * LEAF, LEAF)
        for side, edge, inner, outer in ((0, last, mate(1), next_group), (1, first, mate(GROUP - 1), previous_group)):

            @pl.when(edge == at_edge)
            def _():
                slot = side + 2 * at_edge
                device = outer if at_edge and half == 0 else inner
                for kind, source in enumerate((points.at[:, columns], coefficients.at[columns, :])):
                    part = 2 * half + kind
                    remote(
                        source, near_refs(slot, half)[kind], near_send.at[side, part], near_recv.at[slot, part], device
                    ).start()

    pl.semaphore_wait(barrier, len(partners))
    near_sends(0, 1)

    high, low, norms, ones, rest = parts(points[...] * SCALE)
    right_rows = jnp.concatenate([low, high, high, ones, norms, rest], axis=0).astype(BF16)
    leaf_picks = []
    for leaf in range(2):
        right = right_rows[:, leaf * LEAF : (leaf + 1) * LEAF]
        near_right[2 + leaf] = right
        leaf_picks.append(pick(right, leaf_skeleton[leaf : leaf + 1, :])[0])
    picks = jnp.concatenate(leaf_picks, axis=1)
    node_pick, node_pick_points = pick(picks, node_skeleton[...])
    node_points[4 + place] = node_pick_points
    lane_row = lax.broadcasted_iota(jnp.int32, (1, 128), 1)
    node_lists[place] = jnp.where(
        lane_row == 0, far_list[0, 0], jnp.where(lane_row == 1, far_list[0, 1], far_list[0, 2])
    )
    mine = node_points.at[4 + place]
    for step in (2, 4, 6):
        start(mine, mine, gpts_send.at[step], gpts_recv.at[step], mate(step))
    start(mine, mine, gpts_send.at[0], gpts_recv.at[0], sibling)

    transfer = split(softmax3(exponents(node_pick, picks)))
    for leaf in range(2):
        rows = slice(leaf * LEAF, (leaf + 1) * LEAF)
        half = slice(leaf * RANK, (leaf + 1) * RANK)
        basis = softmax3(exponents(leaf_picks[leaf], near_right[2 + leaf]))
        basis_t = product3(nn, (transfer[0][:, half], transfer[1][:, half]), split(basis))
        basis_t_high[:, rows], basis_t_low[:, rows] = split(basis_t)
        values_high[2 + leaf], values_low[2 + leaf] = split(coefficients[rows, :])
    weights = product3(
        nn,
        (basis_t_high[...], basis_t_low[...]),
        (values_high[2:4].reshape(2 * LEAF, RHS), values_low[2:4].reshape(2 * LEAF, RHS)),
    )
    weights_t[...] = jnp.transpose(weights).reshape(GROUP, SHARE, RANK)
    for step in range(1, GROUP):
        start(
            weights_t.at[lax.rem(place + step, GROUP)],
            node_values.at[4 + place],
            gval_send.at[step],
            gval_recv.at[step],
            mate(step),
        )
    node_values[4 + place] = weights_t[place]
    for step in range(1, GROUP):
        start(node_lists.at[place], node_lists.at[place], glist_send.at[step], glist_recv.at[step], mate(step))

    near_sends(1, 1)
    near_sends(0, 0)
    near_sends(1, 0)

    def near_tile(leaf, half, position):
        rows = pl.ds(pl.multiple_of(leaf * LEAF + half * 256, 256), 256)
        tile = split(jnp.exp2(nn(leaf_left[rows, :], near_right[position])))
        return rows, product3(nn, tile, (values_high[position], values_low[position]))

    for step in (2, 4, 6):
        landed = node_points.at[4 + lax.rem(place + GROUP - step, GROUP)]
        remote(landed, landed, gpts_send.at[step], gpts_recv.at[step], sibling).wait_recv()
        start(landed, landed, gpts_send.at[1 + step], gpts_recv.at[1 + step], sibling)
    landed = node_points.at[4 + sibling_place]
    remote(landed, landed, gpts_send.at[0], gpts_recv.at[0], sibling).wait_recv()
    for step in (2, 4, 6):
        landed = node_points.at[4 + lax.rem(sibling_place + GROUP - step, GROUP)]
        remote(landed, landed, gpts_send.at[1 + step], gpts_recv.at[1 + step], sibling).wait_recv()
    for side, source, target, device in ((0, 8, 0, next_group), (1, 4, 12, previous_group)):
        start(
            node_points.at[pl.ds(source + 2 * core, 2)],
            node_points.at[pl.ds(target + 2 * core, 2)],
            edge_send.at[side],
            edge_recv.at[side],
            device,
        )
    for node in range(4, 12):
        node_right[node] = right_form(node_points[node])

    pair_candidates = [
        jnp.concatenate([node_right[4 + 2 * pair], node_right[5 + 2 * pair]], axis=1) for pair in range(4)
    ]
    for pair in range(4):
        upper_right[pair] = pick(pair_candidates[pair], pair_skeleton[pl.ds(group * 4 + pair, 1), :])[0]
    quad_candidates = [
        jnp.concatenate([upper_right[2 * quad], upper_right[2 * quad + 1]], axis=1) for quad in range(2)
    ]
    for quad in range(2):
        upper_right[4 + quad] = pick(quad_candidates[quad], quad_skeleton[pl.ds(group * 2 + quad, 1), :])[0]
    top_candidates = jnp.concatenate([upper_right[4], upper_right[5]], axis=1)
    top_right, top_picked = pick(top_candidates, top_skeleton[pl.ds(group, 1), :])
    upper_right[6] = top_right
    top_points[core, group] = jnp.where(core == 0, top_picked[0:32], top_picked[32:64])
    share = top_points.at[core, group]
    for step in range(1, TOPS):
        start(share, share, tpts_send.at[step], tpts_recv.at[step], peer(step))
    top_transfer = split(softmax3(exponents(upper_right[6], top_candidates)))
    for quad in range(2):
        half = slice(quad * RANK, (quad + 1) * RANK)
        transfer = split(softmax3(exponents(upper_right[4 + quad], quad_candidates[quad])))
        upper = split(product3(nn, (top_transfer[0][:, half], top_transfer[1][:, half]), transfer))
        for side in range(2):
            pair = 2 * quad + side
            half = slice(side * RANK, (side + 1) * RANK)
            transfer = split(softmax3(exponents(upper_right[pair], pair_candidates[pair])))
            chain = split(product3(nn, (upper[0][:, half], upper[1][:, half]), transfer))
            for child in range(2):
                columns = slice(child * RANK, (child + 1) * RANK)
                chain_high[2 * pair + child] = chain[0][:, columns]
                chain_low[2 * pair + child] = chain[1][:, columns]

    for step in range(1, GROUP):
        source = 4 + lax.rem(place + GROUP - step, GROUP)
        remote(
            weights_t.at[0], node_values.at[source], gval_send.at[step], gval_recv.at[step], mate(step)
        ).wait_recv()
    start(node_values.at[pl.ds(8, 4)], node_values.at[pl.ds(0, 4)], edge_send.at[2], edge_recv.at[2], next_group)
    start(node_values.at[pl.ds(4, 4)], node_values.at[pl.ds(12, 4)], edge_send.at[3], edge_recv.at[3], previous_group)
    pass_on(0)

    total = jnp.zeros((SHARE, RANK), F32)
    for node in range(GROUP):
        total = total + thin_product(nt, node_values[4 + node], (chain_high[node], chain_low[node]))
    top_share[...] = total.reshape(4, SHARE // 4, RANK)
    for step in range(1, TOPS):
        part = top_share.at[lax.rem(group + step, 4)]
        start(part, top_values.at[group], tval_send.at[step], tval_recv.at[step], peer(step))
    top_values[group] = top_share[quarter]

    left_rows = jnp.concatenate([high, low, high, norms, ones, rest], axis=0)
    for leaf in range(2):
        rows = slice(leaf * LEAF, (leaf + 1) * LEAF)
        leaf_left[rows, :] = jnp.transpose(left_rows[:, rows]).astype(BF16)
        for half in range(2):
            tile_rows, value = near_tile(leaf, half, 2 + leaf)
            out[tile_rows, :] = value

    for leaf in range(2):
        rows = slice(leaf * LEAF, (leaf + 1) * LEAF)
        basis_high[rows, :] = jnp.transpose(basis_t_high[:, rows].astype(F32)).astype(BF16)
        basis_low[rows, :] = jnp.transpose(basis_t_low[:, rows].astype(F32)).astype(BF16)
    pass_on(1)

    for side, target in ((0, 0), (1, 12)):
        landed = node_points.at[pl.ds(target + 2 * core, 2)]
        remote(landed, landed, edge_send.at[side], edge_recv.at[side], sibling).wait_recv()
        start(landed, landed, edge_send.at[4 + side], edge_recv.at[4 + side], sibling)
    for step in range(1, GROUP):
        source = lax.rem(place + GROUP - step, GROUP)
        remote(
            node_lists.at[source], node_lists.at[source], glist_send.at[step], glist_recv.at[step], mate(step)
        ).wait_recv()
    to_scalars = pltpu.make_async_copy(node_lists, list_scalars, local_sem)
    to_scalars.start()
    to_scalars.wait()
    for side, target in ((0, 0), (1, 12)):
        landed = node_points.at[pl.ds(target + 2 - 2 * core, 2)]
        remote(landed, landed, edge_send.at[4 + side], edge_recv.at[4 + side], sibling).wait_recv()
    for node in (0, 1, 2, 3, 12, 13, 14, 15):
        node_right[node] = right_form(node_points[node])
    for side, target in ((0, 0), (1, 12)):
        landed = node_values.at[pl.ds(target, 4)]
        remote(landed, landed, edge_send.at[2 + side], edge_recv.at[2 + side], sibling).wait_recv()

    def far_node(node, carry):
        mine_right = node_right[4 + node]
        total = jnp.zeros((SHARE, RANK), F32)
        for slot in range(FAR1):
            entry = list_scalars[node, 0, slot]
            weight = (jnp.minimum(entry, 0) + 1).astype(F32)
            position = jnp.maximum(entry - group * GROUP + 4, 0)
            tile = split(jnp.exp2(exponents(node_right[position], mine_right)))
            total = total + weight * thin_product(nn, node_values[position], tile)
        field_out[node] = total
        return carry

    lax.fori_loop(0, GROUP // 2, far_node, 0, unroll=2)
    for step in range(1, TOPS):
        landed = top_points.at[core, lax.rem(group + TOPS - step, TOPS)]
        remote(landed, landed, tpts_send.at[step], tpts_recv.at[step], sibling).wait_recv()
    start(top_points.at[core], top_points.at[core], tpts_send.at[0], tpts_recv.at[0], sibling)
    lax.fori_loop(GROUP // 2, GROUP, far_node, 0, unroll=2)

    landed = top_points.at[1 - core]
    remote(landed, landed, tpts_send.at[0], tpts_recv.at[0], sibling).wait_recv()

    def top_tiles(target, carry):
        own = right_form(top_points[:, ring_first + target].reshape(FEAT, RANK))
        for slot in range(FAR4):
            source = top_far_list[slot, ring_first + target]
            tile = jnp.exp2(exponents(right_form(top_points[:, source].reshape(FEAT, RANK)), own))
            rows = slice(slot * RANK, (slot + 1) * RANK)
            top_high[target, rows, :], top_low[target, rows, :] = split(tile)
        return carry

    lax.fori_loop(0, 4, top_tiles, 0, unroll=2)
    for step in range(1, TOPS):
        landed = top_values.at[lax.rem(group + TOPS - step, TOPS)]
        remote(landed, landed, tval_send.at[step], tval_recv.at[step], sibling).wait_recv()
    for target in range(4):
        values = jnp.concatenate(
            [top_values[top_far_list[slot, ring_first + target]] for slot in range(FAR4)], axis=1
        )
        high = values.astype(BF16).astype(F32)
        both = jnp.concatenate([high, values - high], axis=0).astype(BF16)
        sums = nn(both, top_high[target]) + nn(both, top_low[target])
        top_out[target] = sums[: SHARE // 4] + sums[SHARE // 4 :]
    for step in range(1, 4):
        start(
            top_out.at[lax.rem(quarter + step, 4)],
            top_in.at[quarter],
            tout_send.at[step],
            tout_recv.at[step],
            ring(step),
        )
    top_in[quarter] = top_out[quarter]
    for step in range(1, 4):
        landed = top_in.at[lax.rem(quarter + 4 - step, 4)]
        remote(landed, landed, tout_send.at[step], tout_recv.at[step], sibling).wait_recv()
    top_field = top_in[...].reshape(SHARE, RANK)
    for node in range(GROUP):
        field_out[node] = field_out[node] + thin_product(nn, top_field, (chain_high[node], chain_low[node]))
    for step in range(1, GROUP):
        start(
            field_out.at[lax.rem(place + step, GROUP)],
            field_in.at[place],
            back_send.at[step],
            back_recv.at[step],
            mate(step),
        )
    field_in[place] = field_out[place]

    for side in range(2):
        for half in range(2):
            for kind, landed in enumerate(near_refs(side, half)):
                part = 2 * half + kind
                remote(landed, landed, near_send.at[side, part], near_recv.at[side, part], sibling).wait_recv()
        for leaf in range(2):
            slot = 4 * side + leaf
            rows = slice(leaf * LEAF, (leaf + 1) * LEAF)
            near_right[slot] = right_form(near_points[side, :, rows] * SCALE)
            values_high[slot], values_low[slot] = split(near_values[side, rows, :])

    def other_tile(step, carry):
        leaf = step // 2
        entry = near_list[leaf, 1 + step % 2]
        position = jnp.maximum(entry - 2 * me + 2, 0)
        weight = (jnp.minimum(entry, 0) + 1).astype(F32)
        for half in range(2):
            rows, value = near_tile(leaf, half, position)
            out[rows, :] = out[rows, :] + weight * value
        return carry

    lax.fori_loop(0, 4, other_tile, 0)

    for step in range(1, GROUP):
        source = lax.rem(place + GROUP - step, GROUP)
        remote(
            field_out.at[0], field_in.at[source], back_send.at[step], back_recv.at[step], mate(step)
        ).wait_recv()
    field = split(jnp.transpose(field_in[...].reshape(RHS, RANK)))
    for quarter in range(4):
        rows = slice(quarter * 256, (quarter + 1) * 256)
        out[rows, :] = out[rows, :] + product3(nn, (basis_high[rows, :], basis_low[rows, :]), field)
    for copy in started:
        copy.wait_send()
    for side in range(2):
        for half in range(2):
            for kind, landed in enumerate(near_refs(side, half)):
                part = 2 * half + kind
                remote(landed, landed, near_send.at[side, part], near_recv.at[side, part], sibling).wait_send()
    for half in range(2):
        for here, path in relays(half):

            @pl.when(here)
            def _():
                for _, copy in path:
                    remote(*copy).wait_send()


def body(
    points,
    coefficients,
    leaf_skeleton,
    node_skeleton,
    pair_skeleton,
    quad_skeleton,
    top_skeleton,
    near_list,
    far_list,
    top_far_list,
):
    vmem = pl.BlockSpec(memory_space=pltpu.VMEM)
    smem = pl.BlockSpec(memory_space=pltpu.SMEM)
    dma = pltpu.SemaphoreType.DMA
    return pl.pallas_call(
        kernel,
        out_shape=jax.ShapeDtypeStruct((2 * LEAF, RHS), F32),
        in_specs=[smem] * 3 + [vmem] * 7,
        out_specs=vmem,
        scratch_shapes=[
            pltpu.VMEM((4, FEAT, 2 * LEAF), F32),
            pltpu.VMEM((4, 2 * LEAF, RHS), F32),
            pltpu.VMEM((16, FEAT, RANK), F32),
            pltpu.VMEM((16, SHARE, RANK), F32),
            pltpu.VMEM((GROUP, 1, 128), jnp.int32),
            pltpu.SMEM((GROUP, 1, 128), jnp.int32),
            pltpu.VMEM((2, TOPS, FEAT // 2, RANK), F32),
            pltpu.VMEM((TOPS, SHARE // 4, RANK), F32),
            pltpu.VMEM((4, SHARE // 4, RANK), F32),
            pltpu.VMEM((4, SHARE // 4, RANK), F32),
            pltpu.VMEM((4, SHARE // 4, RANK), F32),
            pltpu.VMEM((4, FAR4 * RANK, RANK), BF16),
            pltpu.VMEM((4, FAR4 * RANK, RANK), BF16),
            pltpu.VMEM((GROUP, SHARE, RANK), F32),
            pltpu.VMEM((GROUP, SHARE, RANK), F32),
            pltpu.VMEM((GROUP, SHARE, RANK), F32),
            pltpu.VMEM((2 * LEAF, 256), BF16),
            pltpu.VMEM((6, 256, LEAF), BF16),
            pltpu.VMEM((6, LEAF, RHS), BF16),
            pltpu.VMEM((6, LEAF, RHS), BF16),
            pltpu.VMEM((RANK, 2 * LEAF), BF16),
            pltpu.VMEM((RANK, 2 * LEAF), BF16),
            pltpu.VMEM((2 * LEAF, RANK), BF16),
            pltpu.VMEM((2 * LEAF, RANK), BF16),
            pltpu.VMEM((16, 256, RANK), BF16),
            pltpu.VMEM((7, 256, RANK), BF16),
            pltpu.VMEM((GROUP, RANK, RANK), BF16),
            pltpu.VMEM((GROUP, RANK, RANK), BF16),
            dma((2, 4)),
            dma((4, 4)),
            dma((2, 2)),
            dma((GROUP,)),
            dma((GROUP,)),
            dma((GROUP,)),
            dma((GROUP,)),
            dma((GROUP,)),
            dma((GROUP,)),
            dma((6,)),
            dma((6,)),
            dma((TOPS,)),
            dma((TOPS,)),
            dma((TOPS,)),
            dma((TOPS,)),
            dma((4,)),
            dma((4,)),
            dma((GROUP,)),
            dma((GROUP,)),
            dma,
        ],
        compiler_params=pltpu.CompilerParams(
            collective_id=0, has_side_effects=True, vmem_limit_bytes=56 * 1024 * 1024
        ),
    )(
        near_list,
        far_list,
        top_far_list.T,
        points.T,
        coefficients,
        leaf_skeleton,
        node_skeleton,
        pair_skeleton,
        quad_skeleton,
        top_skeleton,
    )


def solution(mesh):
    return jax.shard_map(
        body,
        mesh=mesh,
        in_specs=(
            P("leaf", None),
            P("leaf", None),
            P("leaf", None),
            P("leaf", None),
            P(),
            P(),
            P(),
            P("leaf", None),
            P("leaf", None),
            P(),
        ),
        out_specs=P("leaf", None),
        check_vma=False,
    )
```

```python
import math

import jax
import jax.numpy as jnp
from jax import lax
from jax.experimental import pallas as pl
from jax.experimental.pallas import tpu as pltpu
from jax.sharding import PartitionSpec as P

FEAT = 64
RHS = 256
RANK = 256
LEAF = 512
NEAR = 3
FAR1 = 3
FAR4 = 3
GROUP = 8
TOPS = 16
SHARE = RHS // GROUP
HALF = RANK // 2

MESH = pl.DeviceIdType.MESH
F32 = jnp.float32
BF16 = jnp.bfloat16
SCALE = math.sqrt(2.0 * math.log2(math.e) / FEAT)


def dot(left, right, dims):
    return lax.dot_general(left, right, (dims, ((), ())), preferred_element_type=F32)


def nn(left, right):
    return dot(left, right, ((1,), (0,)))


def nt(left, right):
    return dot(left, right, ((1,), (1,)))


def tn(left, right):
    return dot(left, right, ((0,), (0,)))


def split(values):
    high = values.astype(BF16)
    low = (values - high.astype(F32)).astype(BF16)
    return high, low


def product3(mul, left, right):
    return mul(left[0], right[0]) + (mul(left[0], right[1]) + mul(left[1], right[0]))


def thin_product(mul, left, right):
    rows = left.shape[0]
    high, low = split(left)
    both = mul(jnp.concatenate([high, low], axis=0), right[0])
    return both[:rows] + (both[rows:] + mul(high, right[1]))


def parts(points):
    high = points.astype(BF16).astype(F32)
    low = points - high
    norm = -0.5 * jnp.sum(points * points, axis=0, keepdims=True)
    norm1 = norm.astype(BF16).astype(F32)
    norm2 = (norm - norm1).astype(BF16).astype(F32)
    norm3 = norm - norm1 - norm2
    row = lax.broadcasted_iota(jnp.int32, (16, points.shape[1]), 0)
    norms = jnp.where(row == 0, norm1, jnp.where(row == 1, norm2, jnp.where(row == 2, norm3, 0.0)))
    ones = jnp.where(row < 3, 1.0, 0.0)
    rest = jnp.zeros((32, points.shape[1]), F32)
    return high, low, norms, ones, rest


def right_form(points):
    high, low, norms, ones, rest = parts(points)
    return jnp.concatenate([low, high, high, ones, norms, rest], axis=0).astype(BF16)


def left_of(right):
    return jnp.concatenate(
        [right[64:128], right[0:64], right[128:192], right[208:224], right[192:208], right[224:256]], axis=0
    )


def exponents(left_points, right_points):
    return tn(left_of(left_points), right_points)


def pick(candidates, table_row):
    spread = lax.broadcasted_iota(jnp.int32, (2 * RANK, RANK), 0)
    chosen = jnp.where(spread == table_row, 1.0, 0.0).astype(BF16)
    picked = nn(candidates, chosen)
    return picked.astype(BF16), picked[0:64] + picked[64:128]


def softmax3(exponent):
    top = jnp.max(exponent, axis=0, keepdims=True)
    weights = jnp.exp2(3.0 * (exponent - top))
    return weights / jnp.sum(weights, axis=0, keepdims=True)


def kernel(
    near_list,
    far_list,
    top_far_list,
    points,
    coefficients,
    leaf_skeleton,
    node_skeleton,
    pair_skeleton,
    quad_skeleton,
    top_skeleton,
    out,
    near_points,
    near_values,
    node_points,
    node_values,
    node_lists,
    list_scalars,
    top_points,
    top_values,
    top_share,
    top_out,
    top_in,
    top_high,
    top_low,
    field_out,
    field_in,
    weights_t,
    leaf_left,
    near_right,
    values_high,
    values_low,
    basis_t_high,
    basis_t_low,
    basis_high,
    basis_low,
    node_right,
    upper_right,
    chain_high,
    chain_low,
    near_send,
    near_recv,
    relay_send,
    gpts_send,
    gpts_recv,
    glist_send,
    glist_recv,
    gval_send,
    gval_recv,
    edge_send,
    edge_recv,
    tpts_send,
    tpts_recv,
    tval_send,
    tval_recv,
    tout_send,
    tout_recv,
    back_send,
    back_recv,
    local_sem,
):
    me = lax.axis_index("leaf")
    place = lax.rem(me, GROUP)
    group = me // GROUP
    next_group = lax.rem(group + 1, TOPS) * GROUP + place
    previous_group = lax.rem(group + TOPS - 1, TOPS) * GROUP + place

    core = lax.rem(place, 2)
    sibling_place = place + 1 - 2 * core
    sibling = group * GROUP + sibling_place

    def mate(step):
        return group * GROUP + lax.rem(place + step, GROUP)

    quarter = lax.rem(group, 4)
    ring_first = group - quarter

    def ring(step):
        return (ring_first + lax.rem(quarter + step, 4)) * GROUP + place

    def peer(step):
        return lax.rem(group + step, TOPS) * GROUP + place

    barrier = pltpu.get_barrier_semaphore()
    partners = [mate(step) for step in range(1, GROUP)]
    partners += [peer(step) for step in range(1, TOPS)]
    for partner in partners:
        pl.semaphore_signal(barrier, inc=1, device_id=(partner,), device_id_type=MESH)

    def remote(source, target, send, recv, device):
        return pltpu.make_async_remote_copy(
            src_ref=source, dst_ref=target, send_sem=send, recv_sem=recv, device_id=(device,), device_id_type=MESH
        )

    started = []

    def start(*args):
        copy = remote(*args)
        copy.start()
        started.append(copy)

    def near_refs(slot, half):
        columns = pl.ds(half * LEAF, LEAF)
        return near_points.at[slot, :, columns], near_values.at[slot, columns, :]

    def relay(slot, half, target, device):
        for kind, landed in enumerate(near_refs(slot, half)):
            part = 2 * half + kind
            send = relay_send.at[target, kind]
            yield (
                (landed, landed, send, near_recv.at[slot, part], device),
                (landed, near_refs(target, half)[kind], send, near_recv.at[target, part], device),
            )

    def relays(half):
        if half == 0:
            at_end, at_start = relay(2, 0, 0, mate(1)), relay(3, 0, 1, mate(GROUP - 1))
        else:
            at_end, at_start = relay(3, 1, 1, previous_group), relay(2, 1, 0, next_group)
        return ((place == GROUP - 1, at_end), (place == 0, at_start))

    def pass_on(half):
        for here, path in relays(half):

            @pl.when(here)
            def _():
                for arrived, copy in path:
                    remote(*arrived).wait_recv()
                    remote(*copy).start()

    last = place // (GROUP - 1)
    first = (GROUP - 1 - place) // (GROUP - 1)
    def near_sends(half, at_edge):
        columns = pl.ds(half * LEAF, LEAF)
        for side, edge, inner, outer in ((0, last, mate(1), next_group), (1, first, mate(GROUP - 1), previous_group)):

            @pl.when(edge == at_edge)
            def _():
                slot = side + 2 * at_edge
                device = outer if at_edge and half == 0 else inner
                for kind, source in enumerate((points.at[:, columns], coefficients.at[columns, :])):
                    part = 2 * half + kind
                    remote(
                        source, near_refs(slot, half)[kind], near_send.at[side, part], near_recv.at[slot, part], device
                    ).start()

    pl.semaphore_wait(barrier, len(partners))
    near_sends(0, 1)

    high, low, norms, ones, rest = parts(points[...] * SCALE)
    right_rows = jnp.concatenate([low, high, high, ones, norms, rest], axis=0).astype(BF16)
    leaf_picks = []
    for leaf in range(2):
        right = right_rows[:, leaf * LEAF : (leaf + 1) * LEAF]
        near_right[2 + leaf] = right
        leaf_picks.append(pick(right, leaf_skeleton[leaf : leaf + 1, :])[0])
    picks = jnp.concatenate(leaf_picks, axis=1)
    node_pick, node_pick_points = pick(picks, node_skeleton[...])
    node_points[4 + place] = node_pick_points
    lane_row = lax.broadcasted_iota(jnp.int32, (1, 128), 1)
    node_lists[place] = jnp.where(
        lane_row == 0, far_list[0, 0], jnp.where(lane_row == 1, far_list[0, 1], far_list[0, 2])
    )
    mine = node_points.at[4 + place]
    for step in (2, 4, 6):
        start(mine, mine, gpts_send.at[step], gpts_recv.at[step], mate(step))
    start(mine, mine, gpts_send.at[0], gpts_recv.at[0], sibling)

    transfer = split(softmax3(exponents(node_pick, picks)))
    for leaf in range(2):
        rows = slice(leaf * LEAF, (leaf + 1) * LEAF)
        half = slice(leaf * RANK, (leaf + 1) * RANK)
        basis = softmax3(exponents(leaf_picks[leaf], near_right[2 + leaf]))
        basis_t = product3(nn, (transfer[0][:, half], transfer[1][:, half]), split(basis))
        basis_t_high[:, rows], basis_t_low[:, rows] = split(basis_t)
        values_high[2 + leaf], values_low[2 + leaf] = split(coefficients[rows, :])
    weights = product3(
        nn,
        (basis_t_high[...], basis_t_low[...]),
        (values_high[2:4].reshape(2 * LEAF, RHS), values_low[2:4].reshape(2 * LEAF, RHS)),
    )
    weights_t[...] = jnp.transpose(weights).reshape(GROUP, SHARE, RANK)
    for step in range(1, GROUP):
        start(
            weights_t.at[lax.rem(place + step, GROUP)],
            node_values.at[4 + place],
            gval_send.at[step],
            gval_recv.at[step],
            mate(step),
        )
    node_values[4 + place] = weights_t[place]
    for step in range(1, GROUP):
        start(node_lists.at[place], node_lists.at[place], glist_send.at[step], glist_recv.at[step], mate(step))

    near_sends(1, 1)
    near_sends(0, 0)
    near_sends(1, 0)

    def near_tile(leaf, half, position):
        rows = pl.ds(pl.multiple_of(leaf * LEAF + half * 256, 256), 256)
        tile = split(jnp.exp2(nn(leaf_left[rows, :], near_right[position])))
        return rows, product3(nn, tile, (values_high[position], values_low[position]))

    for step in (2, 4, 6):
        landed = node_points.at[4 + lax.rem(place + GROUP - step, GROUP)]
        remote(landed, landed, gpts_send.at[step], gpts_recv.at[step], sibling).wait_recv()
        start(landed, landed, gpts_send.at[1 + step], gpts_recv.at[1 + step], sibling)
    landed = node_points.at[4 + sibling_place]
    remote(landed, landed, gpts_send.at[0], gpts_recv.at[0], sibling).wait_recv()
    for step in (2, 4, 6):
        landed = node_points.at[4 + lax.rem(sibling_place + GROUP - step, GROUP)]
        remote(landed, landed, gpts_send.at[1 + step], gpts_recv.at[1 + step], sibling).wait_recv()
    for side, source, target, device in ((0, 8, 0, next_group), (1, 4, 12, previous_group)):
        start(
            node_points.at[pl.ds(source + 2 * core, 2)],
            node_points.at[pl.ds(target + 2 * core, 2)],
            edge_send.at[side],
            edge_recv.at[side],
            device,
        )
    for node in range(4, 12):
        node_right[node] = right_form(node_points[node])

    pair_candidates = [
        jnp.concatenate([node_right[4 + 2 * pair], node_right[5 + 2 * pair]], axis=1) for pair in range(4)
    ]
    for pair in range(4):
        upper_right[pair] = pick(pair_candidates[pair], pair_skeleton[pl.ds(group * 4 + pair, 1), :])[0]
    quad_candidates = [
        jnp.concatenate([upper_right[2 * quad], upper_right[2 * quad + 1]], axis=1) for quad in range(2)
    ]
    for quad in range(2):
        upper_right[4 + quad] = pick(quad_candidates[quad], quad_skeleton[pl.ds(group * 2 + quad, 1), :])[0]
    top_candidates = jnp.concatenate([upper_right[4], upper_right[5]], axis=1)
    top_right, top_picked = pick(top_candidates, top_skeleton[pl.ds(group, 1), :])
    upper_right[6] = top_right
    top_points[core, group] = jnp.where(core == 0, top_picked[0:32], top_picked[32:64])
    share = top_points.at[core, group]
    for step in range(1, TOPS):
        start(share, share, tpts_send.at[step], tpts_recv.at[step], peer(step))
    top_transfer = split(softmax3(exponents(upper_right[6], top_candidates)))
    for quad in range(2):
        half = slice(quad * RANK, (quad + 1) * RANK)
        transfer = split(softmax3(exponents(upper_right[4 + quad], quad_candidates[quad])))
        upper = split(product3(nn, (top_transfer[0][:, half], top_transfer[1][:, half]), transfer))
        for side in range(2):
            pair = 2 * quad + side
            half = slice(side * RANK, (side + 1) * RANK)
            transfer = split(softmax3(exponents(upper_right[pair], pair_candidates[pair])))
            chain = split(product3(nn, (upper[0][:, half], upper[1][:, half]), transfer))
            for child in range(2):
                columns = slice(child * RANK, (child + 1) * RANK)
                chain_high[2 * pair + child] = chain[0][:, columns]
                chain_low[2 * pair + child] = chain[1][:, columns]

    for step in range(1, GROUP):
        source = 4 + lax.rem(place + GROUP - step, GROUP)
        remote(
            weights_t.at[0], node_values.at[source], gval_send.at[step], gval_recv.at[step], mate(step)
        ).wait_recv()
    start(node_values.at[pl.ds(8, 4)], node_values.at[pl.ds(0, 4)], edge_send.at[2], edge_recv.at[2], next_group)
    start(node_values.at[pl.ds(4, 4)], node_values.at[pl.ds(12, 4)], edge_send.at[3], edge_recv.at[3], previous_group)
    pass_on(0)

    total = jnp.zeros((SHARE, RANK), F32)
    for node in range(GROUP):
        total = total + thin_product(nt, node_values[4 + node], (chain_high[node], chain_low[node]))
    top_share[...] = total.reshape(4, SHARE // 4, RANK)
    for step in range(1, TOPS):
        part = top_share.at[lax.rem(group + step, 4)]
        start(part, top_values.at[group], tval_send.at[step], tval_recv.at[step], peer(step))
    top_values[group] = top_share[quarter]

    left_rows = jnp.concatenate([high, low, high, norms, ones, rest], axis=0)
    for leaf in range(2):
        rows = slice(leaf * LEAF, (leaf + 1) * LEAF)
        leaf_left[rows, :] = jnp.transpose(left_rows[:, rows]).astype(BF16)
        for half in range(2):
            tile_rows, value = near_tile(leaf, half, 2 + leaf)
            out[tile_rows, :] = value

    for leaf in range(2):
        rows = slice(leaf * LEAF, (leaf + 1) * LEAF)
        basis_high[rows, :] = jnp.transpose(basis_t_high[:, rows].astype(F32)).astype(BF16)
        basis_low[rows, :] = jnp.transpose(basis_t_low[:, rows].astype(F32)).astype(BF16)
    pass_on(1)

    for side, target in ((0, 0), (1, 12)):
        landed = node_points.at[pl.ds(target + 2 * core, 2)]
        remote(landed, landed, edge_send.at[side], edge_recv.at[side], sibling).wait_recv()
        start(landed, landed, edge_send.at[4 + side], edge_recv.at[4 + side], sibling)
    for step in range(1, GROUP):
        source = lax.rem(place + GROUP - step, GROUP)
        remote(
            node_lists.at[source], node_lists.at[source], glist_send.at[step], glist_recv.at[step], mate(step)
        ).wait_recv()
    to_scalars = pltpu.make_async_copy(node_lists, list_scalars, local_sem)
    to_scalars.start()
    to_scalars.wait()
    for side, target in ((0, 0), (1, 12)):
        landed = node_points.at[pl.ds(target + 2 - 2 * core, 2)]
        remote(landed, landed, edge_send.at[4 + side], edge_recv.at[4 + side], sibling).wait_recv()
    for node in (0, 1, 2, 3, 12, 13, 14, 15):
        node_right[node] = right_form(node_points[node])
    for side, target in ((0, 0), (1, 12)):
        landed = node_values.at[pl.ds(target, 4)]
        remote(landed, landed, edge_send.at[2 + side], edge_recv.at[2 + side], sibling).wait_recv()

    def far_node(node, carry):
        mine_right = node_right[4 + node]
        total = jnp.zeros((SHARE, RANK), F32)
        for slot in range(FAR1):
            entry = list_scalars[node, 0, slot]
            weight = (jnp.minimum(entry, 0) + 1).astype(F32)
            position = jnp.maximum(entry - group * GROUP + 4, 0)
            tile = split(jnp.exp2(exponents(node_right[position], mine_right)))
            total = total + weight * thin_product(nn, node_values[position], tile)
        field_out[node] = total
        return carry

    lax.fori_loop(0, GROUP // 2, far_node, 0, unroll=2)
    for step in range(1, TOPS):
        landed = top_points.at[core, lax.rem(group + TOPS - step, TOPS)]
        remote(landed, landed, tpts_send.at[step], tpts_recv.at[step], sibling).wait_recv()
    start(top_points.at[core], top_points.at[core], tpts_send.at[0], tpts_recv.at[0], sibling)

    landed = top_points.at[1 - core]
    remote(landed, landed, tpts_send.at[0], tpts_recv.at[0], sibling).wait_recv()

    def top_tiles(target, carry):
        own = right_form(top_points[:, ring_first + target].reshape(FEAT, RANK))
        for slot in range(FAR4):
            source = top_far_list[slot, ring_first + target]
            tile = jnp.exp2(exponents(right_form(top_points[:, source].reshape(FEAT, RANK)), own))
            rows = slice(slot * RANK, (slot + 1) * RANK)
            top_high[target, rows, :], top_low[target, rows, :] = split(tile)
        return carry

    lax.fori_loop(0, 4, top_tiles, 0, unroll=2)
    for step in range(1, TOPS):
        landed = top_values.at[lax.rem(group + TOPS - step, TOPS)]
        remote(landed, landed, tval_send.at[step], tval_recv.at[step], sibling).wait_recv()
    for target in range(4):
        values = jnp.concatenate(
            [top_values[top_far_list[slot, ring_first + target]] for slot in range(FAR4)], axis=1
        )
        high = values.astype(BF16).astype(F32)
        both = jnp.concatenate([high, values - high], axis=0).astype(BF16)
        sums = nn(both, top_high[target]) + nn(both, top_low[target])
        top_out[target] = sums[: SHARE // 4] + sums[SHARE // 4 :]
    for step in range(1, 4):
        start(
            top_out.at[lax.rem(quarter + step, 4)],
            top_in.at[quarter],
            tout_send.at[step],
            tout_recv.at[step],
            ring(step),
        )
    top_in[quarter] = top_out[quarter]
    lax.fori_loop(GROUP // 2, GROUP, far_node, 0, unroll=2)
    for step in range(1, 4):
        landed = top_in.at[lax.rem(quarter + 4 - step, 4)]
        remote(landed, landed, tout_send.at[step], tout_recv.at[step], sibling).wait_recv()
    top_field = top_in[...].reshape(SHARE, RANK)
    for node in range(GROUP):
        field_out[node] = field_out[node] + thin_product(nn, top_field, (chain_high[node], chain_low[node]))
    for step in range(1, GROUP):
        start(
            field_out.at[lax.rem(place + step, GROUP)],
            field_in.at[place],
            back_send.at[step],
            back_recv.at[step],
            mate(step),
        )
    field_in[place] = field_out[place]

    for turn in range(2):
        side = lax.rem(turn + first, 2)
        for leaf in range(2):
            for kind, landed in enumerate(near_refs(side, leaf)):
                part = 2 * leaf + kind
                remote(landed, landed, near_send.at[side, part], near_recv.at[side, part], sibling).wait_recv()
            slot = 4 * side + leaf
            rows = slice(leaf * LEAF, (leaf + 1) * LEAF)
            near_right[slot] = right_form(near_points[side, :, rows] * SCALE)
            values_high[slot], values_low[slot] = split(near_values[side, rows, :])

    def other_tile(step, carry):
        leaf = step // 2
        entry = near_list[leaf, 1 + step % 2]
        position = jnp.maximum(entry - 2 * me + 2, 0)
        weight = (jnp.minimum(entry, 0) + 1).astype(F32)
        for half in range(2):
            rows, value = near_tile(leaf, half, position)
            out[rows, :] = out[rows, :] + weight * value
        return carry

    lax.fori_loop(0, 4, other_tile, 0)

    for step in range(1, GROUP):
        source = lax.rem(place + GROUP - step, GROUP)
        remote(
            field_out.at[0], field_in.at[source], back_send.at[step], back_recv.at[step], mate(step)
        ).wait_recv()
    field = split(jnp.transpose(field_in[...].reshape(RHS, RANK)))
    for quarter in range(4):
        rows = slice(quarter * 256, (quarter + 1) * 256)
        out[rows, :] = out[rows, :] + product3(nn, (basis_high[rows, :], basis_low[rows, :]), field)
    for copy in started:
        copy.wait_send()
    for side in range(2):
        for half in range(2):
            for kind, landed in enumerate(near_refs(side, half)):
                part = 2 * half + kind
                remote(landed, landed, near_send.at[side, part], near_recv.at[side, part], sibling).wait_send()
    for half in range(2):
        for here, path in relays(half):

            @pl.when(here)
            def _():
                for _, copy in path:
                    remote(*copy).wait_send()


def body(
    points,
    coefficients,
    leaf_skeleton,
    node_skeleton,
    pair_skeleton,
    quad_skeleton,
    top_skeleton,
    near_list,
    far_list,
    top_far_list,
):
    vmem = pl.BlockSpec(memory_space=pltpu.VMEM)
    smem = pl.BlockSpec(memory_space=pltpu.SMEM)
    dma = pltpu.SemaphoreType.DMA
    return pl.pallas_call(
        kernel,
        out_shape=jax.ShapeDtypeStruct((2 * LEAF, RHS), F32),
        in_specs=[smem] * 3 + [vmem] * 7,
        out_specs=vmem,
        scratch_shapes=[
            pltpu.VMEM((4, FEAT, 2 * LEAF), F32),
            pltpu.VMEM((4, 2 * LEAF, RHS), F32),
            pltpu.VMEM((16, FEAT, RANK), F32),
            pltpu.VMEM((16, SHARE, RANK), F32),
            pltpu.VMEM((GROUP, 1, 128), jnp.int32),
            pltpu.SMEM((GROUP, 1, 128), jnp.int32),
            pltpu.VMEM((2, TOPS, FEAT // 2, RANK), F32),
            pltpu.VMEM((TOPS, SHARE // 4, RANK), F32),
            pltpu.VMEM((4, SHARE // 4, RANK), F32),
            pltpu.VMEM((4, SHARE // 4, RANK), F32),
            pltpu.VMEM((4, SHARE // 4, RANK), F32),
            pltpu.VMEM((4, FAR4 * RANK, RANK), BF16),
            pltpu.VMEM((4, FAR4 * RANK, RANK), BF16),
            pltpu.VMEM((GROUP, SHARE, RANK), F32),
            pltpu.VMEM((GROUP, SHARE, RANK), F32),
            pltpu.VMEM((GROUP, SHARE, RANK), F32),
            pltpu.VMEM((2 * LEAF, 256), BF16),
            pltpu.VMEM((6, 256, LEAF), BF16),
            pltpu.VMEM((6, LEAF, RHS), BF16),
            pltpu.VMEM((6, LEAF, RHS), BF16),
            pltpu.VMEM((RANK, 2 * LEAF), BF16),
            pltpu.VMEM((RANK, 2 * LEAF), BF16),
            pltpu.VMEM((2 * LEAF, RANK), BF16),
            pltpu.VMEM((2 * LEAF, RANK), BF16),
            pltpu.VMEM((16, 256, RANK), BF16),
            pltpu.VMEM((7, 256, RANK), BF16),
            pltpu.VMEM((GROUP, RANK, RANK), BF16),
            pltpu.VMEM((GROUP, RANK, RANK), BF16),
            dma((2, 4)),
            dma((4, 4)),
            dma((2, 2)),
            dma((GROUP,)),
            dma((GROUP,)),
            dma((GROUP,)),
            dma((GROUP,)),
            dma((GROUP,)),
            dma((GROUP,)),
            dma((6,)),
            dma((6,)),
            dma((TOPS,)),
            dma((TOPS,)),
            dma((TOPS,)),
            dma((TOPS,)),
            dma((4,)),
            dma((4,)),
            dma((GROUP,)),
            dma((GROUP,)),
            dma,
        ],
        compiler_params=pltpu.CompilerParams(
            collective_id=0, has_side_effects=True, vmem_limit_bytes=56 * 1024 * 1024
        ),
    )(
        near_list,
        far_list,
        top_far_list.T,
        points.T,
        coefficients,
        leaf_skeleton,
        node_skeleton,
        pair_skeleton,
        quad_skeleton,
        top_skeleton,
    )


def solution(mesh):
    return jax.shard_map(
        body,
        mesh=mesh,
        in_specs=(
            P("leaf", None),
            P("leaf", None),
            P("leaf", None),
            P("leaf", None),
            P(),
            P(),
            P(),
            P("leaf", None),
            P("leaf", None),
            P(),
        ),
        out_specs=P("leaf", None),
        check_vma=False,
    )
```
